512 devices in a mesh: dom: 128 (over y, z, core), src: 4 (over x).
Axes of the slice: x: 4, y: 8, z: 8, core: 2. Of those that a mesh axis runs over, the one named last changes fastest.
Arguments:
- adjoint_dofs: float32 [4, 9, 56, 16384], P('src', None, None, 'dom'), may hold values from -6 to 6
- forward_dofs: bfloat16 [4, 9, 56, 16384], P('src', None, None, 'dom'), may hold values from -6 to 6
- star_matrices: float32 [3, 9, 9, 16384], P(None, None, None, 'dom'), may hold values from -3 to 3
- flux_matrices: float32 [4, 2, 9, 9, 16384], P(None, None, None, None, 'dom'), may hold values from -1.5 to 1.5
- stiffness: float32 [3, 56, 56], replicated, may hold values from -0.75 to 0.75
- restriction: float32 [4, 56, 21], replicated, may hold values from -0.75 to 0.75
- rotation: float32 [3, 21, 21], replicated, may hold values from -1.25 to 1.25
- lifting: float32 [4, 21, 56], replicated, may hold values from -0.625 to 0.625
- kernel_weights: float32 [3, 9, 9], replicated, may hold values from -0.046875 to 0.046875
- neighbour: int32 [4, 16384], P(None, 'dom'), may hold values from -1 to 703, as said below
- send_face: int32 [6, 4096], P(None, 'dom'), may hold values from -1 to 511, as said below
- orientation: int32 [4, 16384], P(None, 'dom'), may hold values from 0 to 2
- cluster: int32 [16384], P('dom'), may hold values from 0 to 1
- model_cell: int32 [16384], P('dom'), may hold values from 0 to 16383, as said below
Outputs:
- adjoint_next: float32 [4, 9, 56, 16384], P('src', None, None, 'dom')
- model_gradient: float32 [3, 16384], P(None, 'dom')
The draws below stay inside these ranges and needn't reach their ends.
Inputs may be any that keep to these rules, and one draw needn't show every extreme that they name: Entry [j, p * 128 + e] locates the trace across face j as described in the reference program: h * 128 + e2 for a neighbour in the same partition with its face h, 512 + k * 32 + c for slot c of the faces received from partition p - k - 1 (k < 3) or p + k - 3 + 1 (k >= 3), -1 on the slab's boundary. Faces are paired both ways, and every such slot is listed by the sending partition. `send_face`: row k < 3 of partition p lists in slot c the own face h * 128 + e that borders partition p + k + 1, row 3 + k those bordering p - k - 1; unused slots hold -1. Partition 0 fills all 32 slots of each of its upward rows, and partition 128 - 1 all of each of its downward rows. `model_cell`: the cell of an element of partition p is owned by partition cell // 128, which lies within p - 3 to p + 3; every partition holds elements whose cells are owned by each partition of that range that lies in the slab.
All inputs are finite; a program needn't handle non-finite values.
Results may differ from the reference program's by a relative error of at most 0.0003.
Values sent between devices are 32-bit elements; how exact they have to be, the bound alone decides.
A program may use at most 128 MiB of HBM per device.

```python
import jax
import jax.numpy as jnp
from jax import lax

QUANTITIES = 9
BASIS = 56
FACE_BASIS = 21
PARAMS = 3
REACH = 3
E_DEV = 128
CAP = 32
MCD = 128
SOURCES = 4
E_TOT = 16384
N_DOM = 128


def face_tables(key):
    perm_key = jax.random.fold_in(key, 11)
    count_key = jax.random.fold_in(key, 12)
    faces = 4 * E_DEV
    remote = REACH * CAP
    parts = jnp.arange(N_DOM, dtype=jnp.int32)
    distance = jnp.arange(1, REACH + 1, dtype=jnp.int32)
    counts = jax.random.randint(count_key, (N_DOM, REACH), CAP // 4, CAP + 1)
    counts = counts.at[0].set(CAP)
    counts = jnp.where(parts[:, None] + distance[None, :] == N_DOM - 1, CAP, counts)
    counts = jnp.where(parts[:, None] + distance[None, :] < N_DOM, counts, 0)
    below = parts[:, None] - distance[None, :]
    down_counts = jnp.where(below >= 0, counts[jnp.clip(below, 0, N_DOM - 1), jnp.arange(REACH)[None, :]], 0)
    slots = jnp.arange(CAP, dtype=jnp.int32)
    up_live = slots[None, None, :] < counts[:, :, None]
    down_live = slots[None, None, :] < down_counts[:, :, None]
    perms = jax.vmap(lambda part_id: jax.random.permutation(jax.random.fold_in(perm_key, part_id), faces))(parts).astype(jnp.int32)
    send_up = jnp.where(up_live, perms[:, :remote].reshape(N_DOM, REACH, CAP), -1)
    send_down = jnp.where(down_live, perms[:, remote:2 * remote].reshape(N_DOM, REACH, CAP), -1)
    sending = jnp.concatenate([send_up, send_down], axis=1).astype(jnp.int32)
    places = jnp.argsort(perms, axis=1, stable=True).astype(jnp.int32)
    live_up = jnp.take_along_axis(up_live.reshape(N_DOM, remote), jnp.clip(places, 0, remote - 1), axis=1)
    relative = places - remote
    live_down = jnp.take_along_axis(down_live.reshape(N_DOM, remote), jnp.clip(relative, 0, remote - 1), axis=1)
    partner_pos = 2 * remote + jnp.bitwise_xor(places - 2 * remote, 1)
    partner_face = jnp.take_along_axis(perms, jnp.clip(partner_pos, 0, faces - 1), axis=1)
    upward_value = jnp.where(live_up, faces + remote + places, -1)
    downward_value = jnp.where(live_down, faces + relative, -1)
    values = jnp.where(places >= 2 * remote, partner_face, jnp.where(places < remote, upward_value, downward_value))
    linked = values.reshape(N_DOM, 4, E_DEV).transpose(1, 0, 2).reshape(4, N_DOM * E_DEV).astype(jnp.int32)
    listing = sending.transpose(1, 0, 2).reshape(2 * REACH, N_DOM * CAP).astype(jnp.int32)
    return (linked, listing)


def draw_neighbour(key, part):
    linked, listing = face_tables(key)
    return linked


def draw_send_face(key, part):
    linked, listing = face_tables(key)
    return listing


def draw_model_cell(key, part):
    key = jax.random.fold_in(key, 3)
    first_key = jax.random.fold_in(key, 1)
    second_key = jax.random.fold_in(key, 2)
    element = jnp.arange(E_TOT, dtype=jnp.int32)
    partition = element // E_DEV
    within_part = element % E_DEV
    offset = jax.random.randint(first_key, (E_TOT,), -REACH, REACH + 1)
    offset = jnp.where(within_part < 2 * REACH + 1, within_part - REACH, offset)
    owner = jnp.clip(partition + offset, 0, N_DOM - 1)
    within = jax.random.randint(second_key, (E_TOT,), 0, MCD)
    cells = (owner * MCD + within).astype(jnp.int32)
    cells = cells.at[0].set(0)
    cells = cells.at[E_TOT - 1].set(MCD * N_DOM - 1)
    return cells.astype(jnp.int32)


def plant(values, own_key, least, high):
    shape = values.shape
    place = [jax.random.randint(jax.random.fold_in(own_key, axis), (), 0, shape[axis]) for axis in range(len(shape))]
    values = values.at[tuple(place)].set(least)
    longest = shape.index(max(shape))
    place[longest] = (place[longest] + 1) % shape[longest]
    return values.at[tuple(place)].set(high)


def shard_levels(own_key, dims, cuts, least, largest):
    def one(dim, blocks):
        draws = jax.random.uniform(jax.random.fold_in(jax.random.fold_in(own_key, 6), dim), (blocks,), jnp.float32, least / len(cuts), largest / len(cuts))
        return jnp.repeat(jnp.exp(draws), dims[dim] // blocks).reshape((-1,) + (1,) * (len(dims) - dim - 1))

    loudness = one(*cuts[0])
    for cut in cuts[1:]:
        loudness = loudness * one(*cut)
    return loudness


def bell_draw(rng, shape, spread, most, split=(), kind=jnp.bfloat16):
    factor_of = shard_levels(rng, shape, split, -0.22, 0.18) if split else 1.0
    array = jax.random.normal(rng, shape, jnp.float32) * spread * factor_of
    return jnp.minimum(jnp.maximum(array, -most), most).astype(kind)


def setup_inputs(seed: int = 0) -> dict:
    streams_of = jax.random.split(jax.random.key(seed), 15)
    return {
        "adjoint_dofs": bell_draw(streams_of[0], (SOURCES, QUANTITIES, BASIS, E_TOT), 1.0, 6.0, ((0, 4), (3, 128)), jnp.float32),
        "forward_dofs": bell_draw(streams_of[1], (SOURCES, QUANTITIES, BASIS, E_TOT), 1.0, 6.0, ((0, 4), (3, 128))),
        "star_matrices": bell_draw(streams_of[2], (3, QUANTITIES, QUANTITIES, E_TOT), 0.5, 3.0, ((3, 128),), jnp.float32),
        "flux_matrices": bell_draw(streams_of[3], (4, 2, QUANTITIES, QUANTITIES, E_TOT), 18 ** -0.5, 1.5, ((4, 128),), jnp.float32),
        "stiffness": bell_draw(streams_of[4], (3, BASIS, BASIS), BASIS ** -0.5, 0.75, (), jnp.float32),
        "restriction": bell_draw(streams_of[5], (4, BASIS, FACE_BASIS), BASIS ** -0.5, 0.75, (), jnp.float32),
        "rotation": bell_draw(streams_of[6], (3, FACE_BASIS, FACE_BASIS), FACE_BASIS ** -0.5, 1.25, (), jnp.float32),
        "lifting": bell_draw(streams_of[7], (4, FACE_BASIS, BASIS), 84 ** -0.5, 0.625, (), jnp.float32),
        "kernel_weights": bell_draw(streams_of[8], (PARAMS, QUANTITIES, QUANTITIES), 16384 ** -0.5, 0.046875, (), jnp.float32),
        "neighbour": draw_neighbour(jax.random.fold_in(streams_of[14], 71), 0),
        "send_face": draw_send_face(jax.random.fold_in(streams_of[14], 71), 0),
        "orientation": plant(jax.random.randint(streams_of[11], (4, E_TOT), 0, 3), jax.random.fold_in(streams_of[11], 1), 0, 2).astype(jnp.int32),
        "cluster": plant(jax.random.randint(streams_of[12], (E_TOT,), 0, 2), jax.random.fold_in(streams_of[12], 1), 0, 1).astype(jnp.int32),
        "model_cell": draw_model_cell(jax.random.fold_in(streams_of[14], 71), 0),
    }


precise = lax.Precision.HIGHEST


def predict(state_dofs, stiffness, star_matrices):
    derivative = state_dofs
    integral = state_dofs
    factor = 1.0
    for degree in range(1, 6):
        applied = jnp.einsum("dcb,qbe->dqce", stiffness, derivative, precision=precise)
        derivative = -jnp.einsum("dpqe,dqce->pce", star_matrices, applied, precision=precise)
        factor = factor / (degree + 1)
        integral = integral + factor * derivative
    return integral


def rotate_traces(outside, rotation, orientation):
    result = jnp.zeros_like(outside)
    for position in range(3):
        turned = jnp.einsum("gf,qfje->qgje", rotation[position], outside, precision=precise)
        result = jnp.where(orientation == position, turned, result)
    return result


def reference(adjoint_dofs, forward_dofs, star_matrices, flux_matrices, stiffness, restriction, rotation, lifting, kernel_weights, neighbour, send_face, orientation, cluster, model_cell):
    faces = 4 * E_DEV
    element = jnp.arange(E_TOT, dtype=jnp.int32)
    partition = jnp.broadcast_to(element // E_DEV, (4, E_TOT)).astype(jnp.int32)
    region = jnp.clip((neighbour - faces) // CAP, 0, 2 * REACH - 1).astype(jnp.int32)
    slot_pos = jnp.clip((neighbour - faces) % CAP, 0, CAP - 1).astype(jnp.int32)
    offset = jnp.where(region < REACH, region + 1, REACH - 1 - region)
    source_part = jnp.clip(partition - offset, 0, N_DOM - 1).astype(jnp.int32)
    sent_face = send_face[region, source_part * CAP + slot_pos]
    is_local = neighbour < faces
    global_index = jnp.where(is_local, partition * faces + neighbour, source_part * faces + sent_face)
    present = (neighbour >= 0) & (is_local | (sent_face >= 0))
    global_index = jnp.clip(global_index, 0, faces * N_DOM - 1).astype(jnp.int32).reshape(-1)
    updating = cluster == 0
    width = QUANTITIES * FACE_BASIS

    def one_source(source_pair):
        state_dofs, forward = source_pair
        integral = predict(state_dofs, stiffness, star_matrices)
        traces = jnp.einsum("qbe,jbf->qfje", integral, restriction, precision=precise)
        pooled = traces.reshape(width, 4, N_DOM, E_DEV).transpose(0, 2, 1, 3).reshape(width, faces * N_DOM)
        outside = jnp.take(pooled, global_index, axis=1).reshape(QUANTITIES, FACE_BASIS, 4, E_TOT)
        outside = jnp.where(present, outside, 0.0)
        turned = rotate_traces(outside, rotation, orientation)
        flux_terms = jnp.einsum("jpqe,qfje->pfje", flux_matrices[:, 0], traces, precision=precise)
        flux_terms = flux_terms + jnp.einsum("jpqe,qfje->pfje", flux_matrices[:, 1], turned, precision=precise)
        surface = jnp.einsum("jfb,pfje->pbe", lifting, flux_terms, precision=precise)
        applied = jnp.einsum("dbc,qbe->dqce", stiffness, integral, precision=precise)
        volume = jnp.einsum("dpqe,dqce->pce", star_matrices, applied, precision=precise)
        advanced = jnp.where(updating, state_dofs + volume - surface, state_dofs)
        mixed_field = jnp.einsum("nqr,rbe->nqbe", kernel_weights, forward.astype(jnp.float32), precision=precise)
        kernel_terms = jnp.sum(integral[None] * mixed_field, axis=(1, 2))
        return advanced, kernel_terms

    advanced, kernel_terms = lax.map(one_source, (adjoint_dofs, forward_dofs))
    total_terms = jnp.sum(kernel_terms, axis=0)
    gradient = jax.ops.segment_sum(total_terms.T, model_cell, num_segments=MCD * N_DOM).T
    return advanced, gradient
```

```python
import functools

import jax
import jax.numpy as jnp
from jax import lax
from jax.experimental import pallas as pl
from jax.experimental.pallas import tpu as pltpu
from jax.sharding import PartitionSpec as P

MESH = pl.DeviceIdType.MESH
F32 = jnp.float32
BF16 = jnp.bfloat16

Q = 9
B = 56
BP = 64
F = 21
FP = 24
E = 128
NF = 4
FACES = NF * E
ROWS = 224
QP = Q * FP
PARAMS = 3


def halves(x):
    high = x.astype(BF16).astype(F32)
    return high, x - high


def nt_dot(a, b):
    return lax.dot_general(a, b, (((1,), (1,)), ((), ())), preferred_element_type=F32)


def nn_dot(a, b):
    return jnp.dot(a, b, preferred_element_type=F32)


def kernel(
    n_dom,
    n_src,
    reach,
    cap,
    adj_ref,
    fwd_ref,
    star_ref,
    flux_hbm,
    stiff_ref,
    restr_ref,
    rot_ref,
    lift_ref,
    kw_ref,
    nbr_ref,
    send_ref,
    orient_ref,
    clus_ref,
    cell_ref,
    out_ref,
    grad_ref,
    flux_ref,
    build,
    wk,
    wv,
    wt,
    rb,
    lw,
    v3,
    applied,
    integral,
    fwd32,
    pool,
    pcat,
    oh,
    ohs,
    gath,
    xg,
    turned,
    ft,
    ftb,
    base,
    sendbuf,
    recvbuf,
    sendwin,
    recvwin,
    sendsum,
    recvsum,
    flux_sem,
    send_sem,
    recv_sem,
    wsend_sem,
    wrecv_sem,
    ssend_sem,
    srecv_sem,
):
    dom = lax.axis_index("dom")
    src = lax.axis_index("src")
    slots = 2 * reach
    up = [lax.rem(dom + (k + 1), n_dom) for k in range(reach)]
    down = [lax.rem(dom + (n_dom - k - 1), n_dom) for k in range(reach)]
    partners = up + down
    others = [lax.rem(src + (s + 1), n_src) for s in range(n_src - 1)]

    flux_copy = pltpu.make_async_copy(flux_hbm, flux_ref, flux_sem)
    flux_copy.start()

    barrier = pltpu.get_barrier_semaphore()
    for partner in partners:
        pl.semaphore_signal(barrier, inc=1, device_id={"dom": partner}, device_id_type=MESH)
    for other in others:
        pl.semaphore_signal(barrier, inc=1, device_id={"src": other}, device_id_type=MESH)

    build[...] = jnp.zeros_like(build)
    for d in range(3):
        high, low = halves(stiff_ref[d])
        build[d * B : (d + 1) * B, 0:B] = high
        build[d * B : (d + 1) * B, BP : BP + B] = high
        build[d * B : (d + 1) * B, 2 * BP : 2 * BP + B] = low
    wk[...] = build[0 : 3 * B, 0 : 3 * BP].astype(BF16)

    zeros8 = jnp.zeros((BP - B, E), F32)

    def put_state(q, value):
        high, low = halves(jnp.concatenate([value, zeros8], axis=0))
        lanes = pl.ds(pl.multiple_of(q * E, E), E)
        v3[0:BP, lanes] = high.astype(BF16)
        v3[BP : 2 * BP, lanes] = low.astype(BF16)
        v3[2 * BP : 3 * BP, lanes] = high.astype(BF16)

    def start_state(q, carry):
        value = adj_ref[0, q]
        integral[q] = value
        put_state(q, value)
        return carry

    lax.fori_loop(0, Q, start_state, 0)

    def multiply(weights):
        for tile in range(5):
            lanes = slice(tile * 256, min(tile * 256 + 256, Q * E))
            applied[:, lanes] = nn_dot(weights[...], v3[:, lanes])

    def contract(block, finish):
        p0 = block * 3
        totals = [None] * 3
        for q in range(Q):
            for d in range(3):
                a = applied[d * B : (d + 1) * B, q * E : (q + 1) * E]
                for i in range(3):
                    term = star_ref[p0 + i, q, d : d + 1, :] * a
                    totals[i] = term if totals[i] is None else totals[i] + term
        for i in range(3):
            finish(p0 + i, totals[i])

    def degree_step(k, carry):
        multiply(wk)
        scale = jnp.float32(-1.0 / 6.0)
        for n in range(4):
            scale = jnp.where(k == n, jnp.float32(-1.0 / (n + 2)), scale)

        def finish(p, total):
            value = total * scale
            integral[p] = integral[p] + value
            put_state(p, value)

        def block_step(block, c):
            contract(block, finish)
            return c

        lax.fori_loop(0, 3, block_step, 0)
        return carry

    lax.fori_loop(0, 5, degree_step, 0)

    def take_integral(q, carry):
        put_state(q, integral[q])
        return carry

    lax.fori_loop(0, Q, take_integral, 0)

    build[...] = jnp.zeros_like(build)
    for j in range(NF):
        high, low = halves(restr_ref[:, j, :])
        build[j * FP : j * FP + F, 0:B] = high
        build[j * FP : j * FP + F, BP : BP + B] = high
        build[j * FP : j * FP + F, 2 * BP : 2 * BP + B] = low
    wt[...] = build[0 : NF * FP, 0 : 3 * BP].astype(BF16)
    pool[QP:ROWS, :] = jnp.zeros((ROWS - QP, FACES), F32)
    for tile in range(5):
        wide = min(2, Q - 2 * tile)
        result = nn_dot(wt[...], v3[:, tile * 256 : tile * 256 + wide * E])
        for i in range(wide):
            q = 2 * tile + i
            for j in range(NF):
                pool[q * FP : (q + 1) * FP, j * E : (j + 1) * E] = result[
                    j * FP : (j + 1) * FP, i * E : (i + 1) * E
                ]
    high, low = halves(pool[...])
    pcat[:, 0:FACES] = high.astype(BF16)
    pcat[:, FACES : 2 * FACES] = low.astype(BF16)

    listed = send_ref[...].astype(F32).T
    face_lane = lax.broadcasted_iota(jnp.int32, (cap, FACES), 1).astype(F32)
    for k in range(slots):
        hit = listed[:, k : k + 1] == face_lane
        ohs[k * cap : (k + 1) * cap, :] = jnp.where(hit, 1.0, 0.0).astype(BF16)
    sendbuf[...] = nt_dot(ohs[...], pcat[:, 0:FACES]) + nt_dot(ohs[...], pcat[:, FACES : 2 * FACES])

    pl.semaphore_wait(barrier, 2 * reach + n_src - 1)

    def trace_copy(k):
        part = pl.ds(k * cap, cap)
        return pltpu.make_async_remote_copy(
            src_ref=sendbuf.at[part],
            dst_ref=recvbuf.at[part],
            send_sem=send_sem.at[k],
            recv_sem=recv_sem.at[k],
            device_id={"dom": partners[k]},
            device_id_type=MESH,
        )

    for k in range(slots):
        trace_copy(k).start()

    fwd32[...] = fwd_ref[0].astype(F32)

    def pair_step(q, carry):
        own = integral[q]
        sums = list(carry)
        for r in range(Q):
            product = own * fwd32[r]
            pair = product[0:8]
            for c in range(1, 7):
                pair = pair + product[8 * c : 8 * c + 8]
            for n in range(PARAMS):
                sums[n] = sums[n] + kw_ref[q, n, r] * pair
        return tuple(sums)

    sums = lax.fori_loop(0, Q, pair_step, tuple(jnp.zeros((8, E), F32) for _ in range(PARAMS)))
    terms = jnp.concatenate(
        [jnp.sum(s, axis=0, keepdims=True) for s in sums] + [jnp.zeros((8 - PARAMS, E), F32)], axis=0
    )
    high, low = halves(terms)
    both = jnp.concatenate([high, low], axis=0).astype(BF16)
    place = cell_ref[...] - (dom - reach) * E
    for o in range(2 * reach + 1):
        row = lax.broadcasted_iota(jnp.int32, (E, E), 0) + o * E
        hit = jnp.where(row == place, 1.0, 0.0).astype(BF16)
        summed = nt_dot(both, hit)
        sendwin[o] = summed[0:8] + summed[8:16]

    def window_copy(k):
        o = reach + k + 1 if k < reach else 2 * reach - 1 - k
        return pltpu.make_async_remote_copy(
            src_ref=sendwin.at[o],
            dst_ref=recvwin.at[k],
            send_sem=wsend_sem.at[k],
            recv_sem=wrecv_sem.at[k],
            device_id={"dom": partners[k]},
            device_id_type=MESH,
        )

    for k in range(slots):
        window_copy(k).start()

    flux_copy.wait()

    def flux_side(j, side, values, finish):
        lanes = pl.ds(pl.multiple_of(j * E, E), E)
        x = [values[q * FP : (q + 1) * FP, lanes] for q in range(Q)]
        for p in range(Q):
            total = None
            for q in range(Q):
                term = flux_ref[j, p, q, side : side + 1, :] * x[q]
                total = term if total is None else total + term
            finish(j, p, total)

    def own_step(j, carry):
        def finish(j, p, total):
            ft[pl.ds(pl.multiple_of(j * FP, FP), FP), p * E : (p + 1) * E] = total

        flux_side(j, 0, pool, finish)
        return carry

    lax.fori_loop(0, NF, own_step, 0)

    build[...] = jnp.zeros_like(build)
    for d in range(3):
        high, low = halves(stiff_ref[d].T)
        build[d * B : (d + 1) * B, 0:B] = high
        build[d * B : (d + 1) * B, BP : BP + B] = high
        build[d * B : (d + 1) * B, 2 * BP : 2 * BP + B] = low
    wv[...] = build[0 : 3 * B, 0 : 3 * BP].astype(BF16)
    multiply(wv)

    def volume_step(block, carry):
        def finish(p, total):
            base[p] = adj_ref[0, p] + total

        contract(block, finish)
        return carry

    lax.fori_loop(0, 3, volume_step, 0)

    for j in range(NF):
        row = lax.broadcasted_iota(jnp.int32, (FACES + slots * cap, E), 0)
        hit = row == nbr_ref[j : j + 1, :]
        oh[:, j * E : (j + 1) * E] = jnp.where(hit, 1.0, 0.0).astype(BF16)
    gath[...] = nn_dot(pcat[:, 0:FACES], oh[0:FACES, :]) + nn_dot(pcat[:, FACES : 2 * FACES], oh[0:FACES, :])

    build[...] = jnp.zeros_like(build)
    for o in range(3):
        high, low = halves(rot_ref[o])
        for i in range(3):
            rows = slice(i * 72 + o * FP, i * 72 + o * FP + F)
            build[rows, i * 72 : i * 72 + F] = high
            build[rows, i * 72 + FP : i * 72 + FP + F] = high
            build[rows, i * 72 + 2 * FP : i * 72 + 2 * FP + F] = low
    rb[...] = build[0:QP, 0:ROWS].astype(BF16)
    build[...] = jnp.zeros_like(build)
    for j in range(NF):
        high, low = halves(lift_ref[:, j, :].T)
        build[0:B, j * FP : j * FP + F] = high
        build[0:B, NF * FP + j * FP : NF * FP + j * FP + F] = high
        build[B : 2 * B, j * FP : j * FP + F] = low
    lw[...] = build[0 : 2 * B, 0 : 2 * NF * FP].astype(BF16)

    for k in range(slots):
        window_copy(k).wait_recv()
    total = sendwin[reach]
    for k in range(slots):
        total = total + recvwin[k]
    sendsum[...] = total

    def sum_copy(s):
        return pltpu.make_async_remote_copy(
            src_ref=sendsum,
            dst_ref=recvsum.at[s],
            send_sem=ssend_sem.at[s],
            recv_sem=srecv_sem.at[s],
            device_id={"src": others[s]},
            device_id_type=MESH,
        )

    for s in range(n_src - 1):
        sum_copy(s).start()

    for k in range(slots):
        trace_copy(k).wait_recv()
    high, low = halves(recvbuf[...].T)
    far = oh[FACES : FACES + slots * cap, :]
    gath[...] = gath[...] + nn_dot(high.astype(BF16), far) + nn_dot(low.astype(BF16), far)

    xg[QP:ROWS, :] = jnp.zeros((ROWS - QP, FACES), F32)
    for t in range(3):
        for i in range(3):
            q = 3 * t + i
            high, low = halves(gath[q * FP : (q + 1) * FP, :])
            xg[i * 72 : i * 72 + FP, :] = high
            xg[i * 72 + FP : i * 72 + 2 * FP, :] = low
            xg[i * 72 + 2 * FP : i * 72 + 3 * FP, :] = high
        result = nn_dot(rb[...], xg[...].astype(BF16))
        for i in range(3):
            q = 3 * t + i
            for j in range(NF):
                o = orient_ref[j : j + 1, :]
                r = [
                    result[i * 72 + n * FP : i * 72 + (n + 1) * FP, j * E : (j + 1) * E] for n in range(3)
                ]
                turned[q * FP : (q + 1) * FP, j * E : (j + 1) * E] = jnp.where(
                    o == 0, r[0], jnp.where(o == 1, r[1], r[2])
                )

    def far_step(j, carry):
        def finish(j, p, total):
            rows = pl.ds(pl.multiple_of(j * FP, FP), FP)
            lanes = slice(p * E, (p + 1) * E)
            ft[rows, lanes] = ft[rows, lanes] + total

        flux_side(j, 1, turned, finish)
        return carry

    lax.fori_loop(0, NF, far_step, 0)

    high, low = halves(ft[...])
    ftb[0 : NF * FP, :] = high.astype(BF16)
    ftb[NF * FP : 2 * NF * FP, :] = low.astype(BF16)
    moves = clus_ref[...] == 0
    for tile in range(5):
        wide = min(2, Q - 2 * tile)
        result = nn_dot(lw[...], ftb[:, tile * 256 : tile * 256 + wide * E])
        surface = result[0:B] + result[B : 2 * B]
        for i in range(wide):
            p = 2 * tile + i
            out_ref[0, p] = jnp.where(moves, base[p] - surface[:, i * E : (i + 1) * E], adj_ref[0, p])

    for s in range(n_src - 1):
        sum_copy(s).wait_recv()
    total = sendsum[...]
    for s in range(n_src - 1):
        total = total + recvsum[s]
    grad_ref[...] = total[0:PARAMS]

    for k in range(slots):
        trace_copy(k).wait_send()
        window_copy(k).wait_send()
    for s in range(n_src - 1):
        sum_copy(s).wait_send()


def solution(mesh):
    n_dom, n_src = mesh.shape["dom"], mesh.shape["src"]

    def body(adj, fwd, star, flux, stiff, restr, rot, lift, kw, nbr, send, orient, clus, cell):
        reach, cap = send.shape[0] // 2, send.shape[1]
        star = star.transpose(1, 2, 0, 3)
        flux = flux.transpose(0, 2, 3, 1, 4)
        restr = restr.transpose(2, 0, 1)
        lift = lift.transpose(1, 0, 2)
        kw = kw.transpose(1, 0, 2)
        slots = 2 * reach
        vmem = pl.BlockSpec(memory_space=pltpu.VMEM)
        specs = [vmem] * 14
        specs[3] = pl.BlockSpec(memory_space=pl.ANY)
        specs[8] = pl.BlockSpec(memory_space=pltpu.SMEM)
        dma = pltpu.SemaphoreType.DMA
        return pl.pallas_call(
            functools.partial(kernel, n_dom, n_src, reach, cap),
            out_shape=(
                jax.ShapeDtypeStruct(adj.shape, F32),
                jax.ShapeDtypeStruct((PARAMS, E), F32),
            ),
            in_specs=specs,
            out_specs=(vmem, vmem),
            scratch_shapes=[
                pltpu.VMEM(flux.shape, F32),
                pltpu.VMEM((ROWS, 256), F32),
                pltpu.VMEM((3 * B, 3 * BP), BF16),
                pltpu.VMEM((3 * B, 3 * BP), BF16),
                pltpu.VMEM((NF * FP, 3 * BP), BF16),
                pltpu.VMEM((QP, ROWS), BF16),
                pltpu.VMEM((2 * B, 2 * NF * FP), BF16),
                pltpu.VMEM((3 * BP, Q * E), BF16),
                pltpu.VMEM((3 * B, Q * E), F32),
                pltpu.VMEM((Q, B, E), F32),
                pltpu.VMEM((Q, B, E), F32),
                pltpu.VMEM((ROWS, FACES), F32),
                pltpu.VMEM((ROWS, 2 * FACES), BF16),
                pltpu.VMEM((FACES + slots * cap, FACES), BF16),
                pltpu.VMEM((slots * cap, FACES), BF16),
                pltpu.VMEM((ROWS, FACES), F32),
                pltpu.VMEM((ROWS, FACES), F32),
                pltpu.VMEM((QP, FACES), F32),
                pltpu.VMEM((NF * FP, Q * E), F32),
                pltpu.VMEM((2 * NF * FP, Q * E), BF16),
                pltpu.VMEM((Q, B, E), F32),
                pltpu.VMEM((slots * cap, ROWS), F32),
                pltpu.VMEM((slots * cap, ROWS), F32),
                pltpu.VMEM((slots + 1, 8, E), F32),
                pltpu.VMEM((slots, 8, E), F32),
                pltpu.VMEM((8, E), F32),
                pltpu.VMEM((n_src - 1, 8, E), F32),
                dma,
                dma((slots,)),
                dma((slots,)),
                dma((slots,)),
                dma((slots,)),
                dma((n_src - 1,)),
                dma((n_src - 1,)),
            ],
            compiler_params=pltpu.CompilerParams(
                collective_id=0, has_side_effects=True, vmem_limit_bytes=48 * 1024 * 1024
            ),
        )(
            adj, fwd, star, flux, stiff, restr, rot, lift, kw, nbr, send, orient,
            clus.reshape(1, E), cell.reshape(1, E),
        )

    placed = (
        P("src", None, None, "dom"),
        P("src", None, None, "dom"),
        P(None, None, None, "dom"),
        P(None, None, None, None, "dom"),
        P(),
        P(),
        P(),
        P(),
        P(),
        P(None, "dom"),
        P(None, "dom"),
        P(None, "dom"),
        P("dom"),
        P("dom"),
    )
    return jax.shard_map(
        body,
        mesh=mesh,
        in_specs=placed,
        out_specs=(P("src", None, None, "dom"), P(None, "dom")),
        check_vma=False,
    )
```

```python
import functools

import jax
import jax.numpy as jnp
from jax import lax
from jax.experimental import pallas as pl
from jax.experimental.pallas import tpu as pltpu
from jax.sharding import PartitionSpec as P

MESH = pl.DeviceIdType.MESH
F32 = jnp.float32
BF16 = jnp.bfloat16

Q = 9
B = 56
BP = 64
F = 21
FP = 24
E = 128
NF = 4
FACES = NF * E
ROWS = 224
QP = Q * FP
PARAMS = 3

ADJ, FWD, STAR, FLUX, STIFF, RESTR, ROT, LIFT, KW, NBR, SEND, ORIENT, CLUS, CELL = range(14)


def halves(x):
    high = x.astype(BF16).astype(F32)
    return high, x - high


def nt_dot(a, b):
    return lax.dot_general(a, b, (((1,), (1,)), ((), ())), preferred_element_type=F32)


def nn_dot(a, b):
    return jnp.dot(a, b, preferred_element_type=F32)


def kernel(
    n_dom,
    n_src,
    reach,
    cap,
    *refs,
):
    inputs, (out_ref, grad_ref), refs = refs[:14], refs[14:16], refs[16:]
    held, refs = refs[:14], refs[14:]
    (
        adj_ref, fwd_ref, star_ref, flux_ref, stiff_ref, restr_ref, rot_ref, lift_ref, kw_ref,
        nbr_ref, send_ref, orient_ref, clus_ref, cell_ref,
    ) = held
    (
    build,
    wk,
    wv,
    wt,
    rb,
    lw,
    v3,
    applied,
    integral,
    fwd32,
    pool,
    pcat,
    oh,
    ohs,
    gath,
    xg,
    turned,
    ft,
    ftb,
    base,
    sendbuf,
    recvbuf,
    sendwin,
    recvwin,
    sendsum,
    recvsum,
    load_sem,
    send_sem,
    recv_sem,
    wsend_sem,
    wrecv_sem,
    ssend_sem,
    srecv_sem,
    ) = refs
    dom = lax.axis_index("dom")
    src = lax.axis_index("src")
    slots = 2 * reach
    up = [lax.rem(dom + (k + 1), n_dom) for k in range(reach)]
    down = [lax.rem(dom + (n_dom - k - 1), n_dom) for k in range(reach)]
    partners = up + down
    present = [dom + (k + 1) < n_dom for k in range(reach)] + [dom >= k + 1 for k in range(reach)]
    others = [lax.rem(src + (s + 1), n_src) for s in range(n_src - 1)]

    loads = [pltpu.make_async_copy(inputs[i], held[i], load_sem.at[i]) for i in range(14)]
    for i in (STIFF, ADJ, STAR, RESTR, SEND, FWD, KW, CELL, FLUX, NBR, ROT, LIFT, ORIENT, CLUS):
        loads[i].start()

    barrier = pltpu.get_barrier_semaphore()
    for k in range(slots):

        @pl.when(present[k])
        def _():
            pl.semaphore_signal(barrier, inc=1, device_id={"dom": partners[k]}, device_id_type=MESH)

    for other in others:
        pl.semaphore_signal(barrier, inc=1, device_id={"src": other}, device_id_type=MESH)

    build[...] = jnp.zeros_like(build)
    loads[STIFF].wait()
    for d in range(3):
        high, low = halves(stiff_ref[d])
        build[d * B : (d + 1) * B, 0:B] = high
        build[d * B : (d + 1) * B, BP : BP + B] = high
        build[d * B : (d + 1) * B, 2 * BP : 2 * BP + B] = low
    wk[...] = build[0 : 3 * B, 0 : 3 * BP].astype(BF16)

    zeros8 = jnp.zeros((BP - B, E), F32)

    def put_state(q, value):
        high, low = halves(jnp.concatenate([value, zeros8], axis=0))
        lanes = pl.ds(pl.multiple_of(q * E, E), E)
        v3[0:BP, lanes] = high.astype(BF16)
        v3[BP : 2 * BP, lanes] = low.astype(BF16)
        v3[2 * BP : 3 * BP, lanes] = high.astype(BF16)

    def start_state(q, carry):
        value = adj_ref[0, q]
        integral[q] = value
        put_state(q, value)
        return carry

    loads[ADJ].wait()
    lax.fori_loop(0, Q, start_state, 0)
    loads[STAR].wait()

    def multiply(weights):
        for tile in range(5):
            lanes = slice(tile * 256, min(tile * 256 + 256, Q * E))
            applied[:, lanes] = nn_dot(weights[...], v3[:, lanes])

    def contract(block, finish):
        p0 = block * 3
        totals = [None] * 3
        for q in range(Q):
            for d in range(3):
                a = applied[d * B : (d + 1) * B, q * E : (q + 1) * E]
                for i in range(3):
                    term = star_ref[p0 + i, q, d : d + 1, :] * a
                    totals[i] = term if totals[i] is None else totals[i] + term
        for i in range(3):
            finish(p0 + i, totals[i])

    def degree_step(k, carry):
        multiply(wk)
        scale = jnp.float32(-1.0 / 6.0)
        for n in range(4):
            scale = jnp.where(k == n, jnp.float32(-1.0 / (n + 2)), scale)

        def finish(p, total):
            value = total * scale
            integral[p] = integral[p] + value
            put_state(p, value)

        def block_step(block, c):
            contract(block, finish)
            return c

        lax.fori_loop(0, 3, block_step, 0)
        return carry

    lax.fori_loop(0, 5, degree_step, 0)

    def take_integral(q, carry):
        put_state(q, integral[q])
        return carry

    lax.fori_loop(0, Q, take_integral, 0)

    loads[RESTR].wait()
    build[...] = jnp.zeros_like(build)
    for j in range(NF):
        high, low = halves(restr_ref[:, j, :])
        build[j * FP : j * FP + F, 0:B] = high
        build[j * FP : j * FP + F, BP : BP + B] = high
        build[j * FP : j * FP + F, 2 * BP : 2 * BP + B] = low
    wt[...] = build[0 : NF * FP, 0 : 3 * BP].astype(BF16)
    pool[QP:ROWS, :] = jnp.zeros((ROWS - QP, FACES), F32)
    for tile in range(5):
        wide = min(2, Q - 2 * tile)
        result = nn_dot(wt[...], v3[:, tile * 256 : tile * 256 + wide * E])
        for i in range(wide):
            q = 2 * tile + i
            for j in range(NF):
                pool[q * FP : (q + 1) * FP, j * E : (j + 1) * E] = result[
                    j * FP : (j + 1) * FP, i * E : (i + 1) * E
                ]
    high, low = halves(pool[...])
    pcat[:, 0:FACES] = high.astype(BF16)
    pcat[:, FACES : 2 * FACES] = low.astype(BF16)

    loads[SEND].wait()
    listed = send_ref[...].astype(F32).T
    face_lane = lax.broadcasted_iota(jnp.int32, (cap, FACES), 1).astype(F32)
    for k in range(slots):
        hit = listed[:, k : k + 1] == face_lane
        ohs[k * cap : (k + 1) * cap, :] = jnp.where(hit, 1.0, 0.0).astype(BF16)
    sendbuf[...] = nt_dot(ohs[...], pcat[:, 0:FACES]) + nt_dot(ohs[...], pcat[:, FACES : 2 * FACES])

    arrivals = n_src - 1
    for k in range(slots):
        arrivals = arrivals + present[k].astype(jnp.int32)
    pl.semaphore_wait(barrier, arrivals)

    def trace_copy(k):
        part = pl.ds(k * cap, cap)
        return pltpu.make_async_remote_copy(
            src_ref=sendbuf.at[part],
            dst_ref=recvbuf.at[part],
            send_sem=send_sem.at[k],
            recv_sem=recv_sem.at[k],
            device_id={"dom": partners[k]},
            device_id_type=MESH,
        )

    for k in range(slots):

        @pl.when(present[k])
        def _():
            trace_copy(k).start()


    for i in (FWD, KW, CELL):
        loads[i].wait()
    fwd32[...] = fwd_ref[0].astype(F32)

    def pair_step(q, carry):
        own = integral[q]
        sums = list(carry)
        for r in range(Q):
            product = own * fwd32[r]
            pair = product[0:8]
            for c in range(1, 7):
                pair = pair + product[8 * c : 8 * c + 8]
            for n in range(PARAMS):
                sums[n] = sums[n] + kw_ref[q, n, r] * pair
        return tuple(sums)

    sums = lax.fori_loop(0, Q, pair_step, tuple(jnp.zeros((8, E), F32) for _ in range(PARAMS)))
    terms = jnp.concatenate(
        [jnp.sum(s, axis=0, keepdims=True) for s in sums] + [jnp.zeros((8 - PARAMS, E), F32)], axis=0
    )
    high, low = halves(terms)
    both = jnp.concatenate([high, low], axis=0).astype(BF16)
    place = cell_ref[...] - (dom - reach) * E
    for o in range(2 * reach + 1):
        row = lax.broadcasted_iota(jnp.int32, (E, E), 0) + o * E
        hit = jnp.where(row == place, 1.0, 0.0).astype(BF16)
        summed = nt_dot(both, hit)
        sendwin[o] = summed[0:8] + summed[8:16]

    def window_copy(k):
        o = reach + k + 1 if k < reach else 2 * reach - 1 - k
        return pltpu.make_async_remote_copy(
            src_ref=sendwin.at[o],
            dst_ref=recvwin.at[k],
            send_sem=wsend_sem.at[k],
            recv_sem=wrecv_sem.at[k],
            device_id={"dom": partners[k]},
            device_id_type=MESH,
        )

    for k in range(slots):

        @pl.when(present[k])
        def _():
            window_copy(k).start()


    for i in (FLUX, NBR, ROT, LIFT, ORIENT, CLUS):
        loads[i].wait()

    def flux_side(j, side, values, finish):
        lanes = pl.ds(pl.multiple_of(j * E, E), E)
        x = [values[q * FP : (q + 1) * FP, lanes] for q in range(Q)]
        for p in range(Q):
            total = None
            for q in range(Q):
                term = flux_ref[j, p, q, side : side + 1, :] * x[q]
                total = term if total is None else total + term
            finish(j, p, total)

    def own_step(j, carry):
        def finish(j, p, total):
            ft[pl.ds(pl.multiple_of(j * FP, FP), FP), p * E : (p + 1) * E] = total

        flux_side(j, 0, pool, finish)
        return carry

    lax.fori_loop(0, NF, own_step, 0)

    build[...] = jnp.zeros_like(build)
    for d in range(3):
        high, low = halves(stiff_ref[d].T)
        build[d * B : (d + 1) * B, 0:B] = high
        build[d * B : (d + 1) * B, BP : BP + B] = high
        build[d * B : (d + 1) * B, 2 * BP : 2 * BP + B] = low
    wv[...] = build[0 : 3 * B, 0 : 3 * BP].astype(BF16)
    multiply(wv)

    def volume_step(block, carry):
        def finish(p, total):
            base[p] = adj_ref[0, p] + total

        contract(block, finish)
        return carry

    lax.fori_loop(0, 3, volume_step, 0)

    for j in range(NF):
        row = lax.broadcasted_iota(jnp.int32, (FACES + slots * cap, E), 0)
        hit = row == nbr_ref[j : j + 1, :]
        oh[:, j * E : (j + 1) * E] = jnp.where(hit, 1.0, 0.0).astype(BF16)
    gath[...] = nn_dot(pcat[:, 0:FACES], oh[0:FACES, :]) + nn_dot(pcat[:, FACES : 2 * FACES], oh[0:FACES, :])

    build[...] = jnp.zeros_like(build)
    for o in range(3):
        high, low = halves(rot_ref[o])
        for i in range(3):
            rows = slice(i * 72 + o * FP, i * 72 + o * FP + F)
            build[rows, i * 72 : i * 72 + F] = high
            build[rows, i * 72 + FP : i * 72 + FP + F] = high
            build[rows, i * 72 + 2 * FP : i * 72 + 2 * FP + F] = low
    rb[...] = build[0:QP, 0:ROWS].astype(BF16)
    build[...] = jnp.zeros_like(build)
    for j in range(NF):
        high, low = halves(lift_ref[:, j, :].T)
        build[0:B, j * FP : j * FP + F] = high
        build[0:B, NF * FP + j * FP : NF * FP + j * FP + F] = high
        build[B : 2 * B, j * FP : j * FP + F] = low
    lw[...] = build[0 : 2 * B, 0 : 2 * NF * FP].astype(BF16)

    for k in range(slots):

        @pl.when(present[(k + reach) % slots])
        def _():
            window_copy(k).wait_recv()

        @pl.when(jnp.logical_not(present[(k + reach) % slots]))
        def _():
            recvwin[k] = jnp.zeros((8, E), F32)

    total = sendwin[reach]
    for k in range(slots):
        total = total + recvwin[k]
    sendsum[...] = total

    def sum_copy(s):
        return pltpu.make_async_remote_copy(
            src_ref=sendsum,
            dst_ref=recvsum.at[s],
            send_sem=ssend_sem.at[s],
            recv_sem=srecv_sem.at[s],
            device_id={"src": others[s]},
            device_id_type=MESH,
        )

    for s in range(n_src - 1):
        sum_copy(s).start()

    for k in range(slots):

        @pl.when(present[(k + reach) % slots])
        def _():
            trace_copy(k).wait_recv()

        @pl.when(jnp.logical_not(present[(k + reach) % slots]))
        def _():
            recvbuf[k * cap : (k + 1) * cap] = jnp.zeros((cap, ROWS), F32)

    high, low = halves(recvbuf[...].T)
    far = oh[FACES : FACES + slots * cap, :]
    gath[...] = gath[...] + nn_dot(high.astype(BF16), far) + nn_dot(low.astype(BF16), far)

    xg[QP:ROWS, :] = jnp.zeros((ROWS - QP, FACES), F32)
    for t in range(3):
        for i in range(3):
            q = 3 * t + i
            high, low = halves(gath[q * FP : (q + 1) * FP, :])
            xg[i * 72 : i * 72 + FP, :] = high
            xg[i * 72 + FP : i * 72 + 2 * FP, :] = low
            xg[i * 72 + 2 * FP : i * 72 + 3 * FP, :] = high
        result = nn_dot(rb[...], xg[...].astype(BF16))
        for i in range(3):
            q = 3 * t + i
            for j in range(NF):
                o = orient_ref[j : j + 1, :]
                r = [
                    result[i * 72 + n * FP : i * 72 + (n + 1) * FP, j * E : (j + 1) * E] for n in range(3)
                ]
                turned[q * FP : (q + 1) * FP, j * E : (j + 1) * E] = jnp.where(
                    o == 0, r[0], jnp.where(o == 1, r[1], r[2])
                )

    def far_step(j, carry):
        def finish(j, p, total):
            rows = pl.ds(pl.multiple_of(j * FP, FP), FP)
            lanes = slice(p * E, (p + 1) * E)
            ft[rows, lanes] = ft[rows, lanes] + total

        flux_side(j, 1, turned, finish)
        return carry

    lax.fori_loop(0, NF, far_step, 0)

    high, low = halves(ft[...])
    ftb[0 : NF * FP, :] = high.astype(BF16)
    ftb[NF * FP : 2 * NF * FP, :] = low.astype(BF16)
    moves = clus_ref[...] == 0
    for tile in range(5):
        wide = min(2, Q - 2 * tile)
        result = nn_dot(lw[...], ftb[:, tile * 256 : tile * 256 + wide * E])
        surface = result[0:B] + result[B : 2 * B]
        for i in range(wide):
            p = 2 * tile + i
            out_ref[0, p] = jnp.where(moves, base[p] - surface[:, i * E : (i + 1) * E], adj_ref[0, p])

    for s in range(n_src - 1):
        sum_copy(s).wait_recv()
    total = sendsum[...]
    for s in range(n_src - 1):
        total = total + recvsum[s]
    grad_ref[...] = total[0:PARAMS]

    for k in range(slots):

        @pl.when(present[k])
        def _():
            trace_copy(k).wait_send()
            window_copy(k).wait_send()

    for s in range(n_src - 1):
        sum_copy(s).wait_send()


def solution(mesh):
    n_dom, n_src = mesh.shape["dom"], mesh.shape["src"]

    def body(adj, fwd, star, flux, stiff, restr, rot, lift, kw, nbr, send, orient, clus, cell):
        reach, cap = send.shape[0] // 2, send.shape[1]
        star = star.transpose(1, 2, 0, 3)
        flux = flux.transpose(0, 2, 3, 1, 4)
        restr = restr.transpose(2, 0, 1)
        lift = lift.transpose(1, 0, 2)
        kw = kw.transpose(1, 0, 2)
        slots = 2 * reach
        operands = (
            adj, fwd, star, flux, stiff, restr, rot, lift, kw, nbr, send, orient,
            clus.reshape(1, E), cell.reshape(1, E),
        )
        vmem = pl.BlockSpec(memory_space=pltpu.VMEM)
        dma = pltpu.SemaphoreType.DMA
        return pl.pallas_call(
            functools.partial(kernel, n_dom, n_src, reach, cap),
            out_shape=(
                jax.ShapeDtypeStruct(adj.shape, F32),
                jax.ShapeDtypeStruct((PARAMS, E), F32),
            ),
            in_specs=[pl.BlockSpec(memory_space=pltpu.HBM)] * 14,
            out_specs=(vmem, vmem),
            scratch_shapes=[
                *[(pltpu.SMEM if i == KW else pltpu.VMEM)(x.shape, x.dtype) for i, x in enumerate(operands)],
                pltpu.VMEM((ROWS, 256), F32),
                pltpu.VMEM((3 * B, 3 * BP), BF16),
                pltpu.VMEM((3 * B, 3 * BP), BF16),
                pltpu.VMEM((NF * FP, 3 * BP), BF16),
                pltpu.VMEM((QP, ROWS), BF16),
                pltpu.VMEM((2 * B, 2 * NF * FP), BF16),
                pltpu.VMEM((3 * BP, Q * E), BF16),
                pltpu.VMEM((3 * B, Q * E), F32),
                pltpu.VMEM((Q, B, E), F32),
                pltpu.VMEM((Q, B, E), F32),
                pltpu.VMEM((ROWS, FACES), F32),
                pltpu.VMEM((ROWS, 2 * FACES), BF16),
                pltpu.VMEM((FACES + slots * cap, FACES), BF16),
                pltpu.VMEM((slots * cap, FACES), BF16),
                pltpu.VMEM((ROWS, FACES), F32),
                pltpu.VMEM((ROWS, FACES), F32),
                pltpu.VMEM((QP, FACES), F32),
                pltpu.VMEM((NF * FP, Q * E), F32),
                pltpu.VMEM((2 * NF * FP, Q * E), BF16),
                pltpu.VMEM((Q, B, E), F32),
                pltpu.VMEM((slots * cap, ROWS), F32),
                pltpu.VMEM((slots * cap, ROWS), F32),
                pltpu.VMEM((slots + 1, 8, E), F32),
                pltpu.VMEM((slots, 8, E), F32),
                pltpu.VMEM((8, E), F32),
                pltpu.VMEM((n_src - 1, 8, E), F32),
                dma((14,)),
                dma((slots,)),
                dma((slots,)),
                dma((slots,)),
                dma((slots,)),
                dma((n_src - 1,)),
                dma((n_src - 1,)),
            ],
            compiler_params=pltpu.CompilerParams(
                collective_id=0, has_side_effects=True, vmem_limit_bytes=63 * 1024 * 1024
            ),
        )(*operands)

    placed = (
        P("src", None, None, "dom"),
        P("src", None, None, "dom"),
        P(None, None, None, "dom"),
        P(None, None, None, None, "dom"),
        P(),
        P(),
        P(),
        P(),
        P(),
        P(None, "dom"),
        P(None, "dom"),
        P(None, "dom"),
        P("dom"),
        P("dom"),
    )
    return jax.shard_map(
        body,
        mesh=mesh,
        in_specs=placed,
        out_specs=(P("src", None, None, "dom"), P(None, "dom")),
        check_vma=False,
    )
```

```python
import functools

import jax
import jax.numpy as jnp
from jax import lax
from jax.experimental import pallas as pl
from jax.experimental.pallas import tpu as pltpu
from jax.sharding import PartitionSpec as P

MESH = pl.DeviceIdType.MESH
F32 = jnp.float32
BF16 = jnp.bfloat16

Q = 9
B = 56
BP = 64
F = 21
FP = 24
E = 128
NF = 4
FACES = NF * E
ROWS = 224
QP = Q * FP
PARAMS = 3

ADJ, FWD, STAR, FLUX, STIFF, RESTR, ROT, LIFT, KW, NBR, SEND, ORIENT, CLUS, CELL = range(14)


def halves(x):
    high = x.astype(BF16).astype(F32)
    return high, x - high


def nt_dot(a, b):
    return lax.dot_general(a, b, (((1,), (1,)), ((), ())), preferred_element_type=F32)


def nn_dot(a, b):
    return jnp.dot(a, b, preferred_element_type=F32)


def kernel(
    n_dom,
    n_src,
    reach,
    cap,
    *refs,
):
    inputs, (out_ref, grad_ref), refs = refs[:14], refs[14:16], refs[16:]
    held, refs = refs[:14], refs[14:]
    (
        adj_ref, fwd_ref, star_ref, flux_ref, stiff_ref, restr_ref, rot_ref, lift_ref, kw_ref,
        nbr_ref, send_ref, orient_ref, clus_ref, cell_ref,
    ) = held
    (
    build,
    wk,
    wv,
    wt,
    rb,
    lw,
    v3,
    applied,
    integral,
    fwd32,
    pool,
    pcat,
    oh,
    ohs,
    gath,
    xg,
    turned,
    ft,
    ftb,
    base,
    sendbuf,
    recvbuf,
    sendwin,
    recvwin,
    load_sem,
    send_sem,
    recv_sem,
    wsend_sem,
    wrecv_sem,
    ) = refs
    dom = lax.axis_index("dom")
    src = lax.axis_index("src")
    slots = 2 * reach
    offsets = [o - reach for o in range(2 * reach + 1)]
    present = [(dom + d >= 0) & (dom + d < n_dom) for d in offsets]
    sources = [lax.rem(src + s, n_src) for s in range(n_src)]
    goes = [reach + k + 1 for k in range(reach)] + [reach - k - 1 for k in range(reach)]
    comes = [2 * reach - o for o in goes]
    windows = [(o, s) for o in range(2 * reach + 1) for s in range(n_src) if (o, s) != (reach, 0)]

    def for_each(keys, where, action):
        for o in range(2 * reach + 1):
            mine = [k for k in keys if where(k) == o]
            if not mine:
                continue

            @pl.when(present[o])
            def _():
                for k in mine:
                    action(k)

    loads = [pltpu.make_async_copy(inputs[i], held[i], load_sem.at[i]) for i in range(14)]
    for i in (STIFF, ADJ, STAR, RESTR, SEND, FWD, KW, CELL, FLUX, NBR, ROT, LIFT, ORIENT, CLUS):
        loads[i].start()

    barrier = pltpu.get_barrier_semaphore()

    def greet(key):
        o, s = key
        pl.semaphore_signal(
            barrier, inc=1, device_id={"dom": dom + offsets[o], "src": sources[s]}, device_id_type=MESH
        )

    for_each(windows, lambda key: key[0], greet)

    build[...] = jnp.zeros_like(build)
    loads[STIFF].wait()
    for d in range(3):
        high, low = halves(stiff_ref[d])
        build[d * B : (d + 1) * B, 0:B] = high
        build[d * B : (d + 1) * B, BP : BP + B] = high
        build[d * B : (d + 1) * B, 2 * BP : 2 * BP + B] = low
    wk[...] = build[0 : 3 * B, 0 : 3 * BP].astype(BF16)

    zeros8 = jnp.zeros((BP - B, E), F32)

    def put_state(q, value):
        high, low = halves(jnp.concatenate([value, zeros8], axis=0))
        lanes = pl.ds(pl.multiple_of(q * E, E), E)
        v3[0:BP, lanes] = high.astype(BF16)
        v3[BP : 2 * BP, lanes] = low.astype(BF16)
        v3[2 * BP : 3 * BP, lanes] = high.astype(BF16)

    def start_state(q, carry):
        value = adj_ref[0, q]
        integral[q] = value
        put_state(q, value)
        return carry

    loads[ADJ].wait()
    lax.fori_loop(0, Q, start_state, 0)
    loads[STAR].wait()

    def multiply(weights):
        for tile in range(5):
            lanes = slice(tile * 256, min(tile * 256 + 256, Q * E))
            applied[:, lanes] = nn_dot(weights[...], v3[:, lanes])

    def contract(block, finish):
        p0 = block * 3
        totals = [None] * 3
        for q in range(Q):
            for d in range(3):
                a = applied[d * B : (d + 1) * B, q * E : (q + 1) * E]
                for i in range(3):
                    term = star_ref[p0 + i, q, d : d + 1, :] * a
                    totals[i] = term if totals[i] is None else totals[i] + term
        for i in range(3):
            finish(p0 + i, totals[i])

    def degree_step(k, carry):
        multiply(wk)
        scale = jnp.float32(-1.0 / 6.0)
        for n in range(4):
            scale = jnp.where(k == n, jnp.float32(-1.0 / (n + 2)), scale)

        def finish(p, total):
            value = total * scale
            integral[p] = integral[p] + value
            put_state(p, value)

        def block_step(block, c):
            contract(block, finish)
            return c

        lax.fori_loop(0, 3, block_step, 0)
        return carry

    lax.fori_loop(0, 5, degree_step, 0)

    for i in (FWD, KW, CELL):
        loads[i].wait()
    fwd32[...] = fwd_ref[0].astype(F32)

    def pair_step(q, carry):
        own = integral[q]
        sums = list(carry)
        for r in range(Q):
            product = own * fwd32[r]
            pair = product[0:8]
            for c in range(1, 7):
                pair = pair + product[8 * c : 8 * c + 8]
            for n in range(PARAMS):
                sums[n] = sums[n] + kw_ref[q, n, r] * pair
        return tuple(sums)

    sums = lax.fori_loop(0, Q, pair_step, tuple(jnp.zeros((8, E), F32) for _ in range(PARAMS)))
    terms = jnp.concatenate(
        [jnp.sum(s, axis=0, keepdims=True) for s in sums] + [jnp.zeros((8 - PARAMS, E), F32)], axis=0
    )
    high, low = halves(terms)
    both = jnp.concatenate([high, low], axis=0).astype(BF16)
    place = cell_ref[...] - (dom - reach) * E
    for o in range(2 * reach + 1):
        row = lax.broadcasted_iota(jnp.int32, (E, E), 0) + o * E
        hit = jnp.where(row == place, 1.0, 0.0).astype(BF16)
        summed = nt_dot(both, hit)
        sendwin[o] = summed[0:8] + summed[8:16]

    neighbours = -1
    for here in present:
        neighbours = neighbours + n_src * here.astype(jnp.int32)
    pl.semaphore_wait(barrier, neighbours)

    def window_copy(n):
        o, s = windows[n]
        return pltpu.make_async_remote_copy(
            src_ref=sendwin.at[o],
            dst_ref=recvwin.at[n],
            send_sem=wsend_sem.at[n],
            recv_sem=wrecv_sem.at[n],
            device_id={"dom": dom + offsets[o], "src": sources[s]},
            device_id_type=MESH,
        )

    count = range(len(windows))
    for_each(count, lambda n: windows[n][0], lambda n: window_copy(n).start())

    def take_integral(q, carry):
        put_state(q, integral[q])
        return carry

    lax.fori_loop(0, Q, take_integral, 0)

    loads[RESTR].wait()
    build[...] = jnp.zeros_like(build)
    for j in range(NF):
        high, low = halves(restr_ref[:, j, :])
        build[j * FP : j * FP + F, 0:B] = high
        build[j * FP : j * FP + F, BP : BP + B] = high
        build[j * FP : j * FP + F, 2 * BP : 2 * BP + B] = low
    wt[...] = build[0 : NF * FP, 0 : 3 * BP].astype(BF16)
    pool[QP:ROWS, :] = jnp.zeros((ROWS - QP, FACES), F32)
    for tile in range(5):
        wide = min(2, Q - 2 * tile)
        result = nn_dot(wt[...], v3[:, tile * 256 : tile * 256 + wide * E])
        for i in range(wide):
            q = 2 * tile + i
            for j in range(NF):
                pool[q * FP : (q + 1) * FP, j * E : (j + 1) * E] = result[
                    j * FP : (j + 1) * FP, i * E : (i + 1) * E
                ]
    high, low = halves(pool[...])
    pcat[:, 0:FACES] = high.astype(BF16)
    pcat[:, FACES : 2 * FACES] = low.astype(BF16)

    loads[SEND].wait()
    listed = send_ref[...].astype(F32).T
    face_lane = lax.broadcasted_iota(jnp.int32, (cap, FACES), 1).astype(F32)
    for k in range(slots):
        hit = listed[:, k : k + 1] == face_lane
        ohs[k * cap : (k + 1) * cap, :] = jnp.where(hit, 1.0, 0.0).astype(BF16)
    sendbuf[...] = nt_dot(ohs[...], pcat[:, 0:FACES]) + nt_dot(ohs[...], pcat[:, FACES : 2 * FACES])

    def trace_copy(k):
        part = pl.ds(k * cap, cap)
        return pltpu.make_async_remote_copy(
            src_ref=sendbuf.at[part],
            dst_ref=recvbuf.at[part],
            send_sem=send_sem.at[k],
            recv_sem=recv_sem.at[k],
            device_id={"dom": dom + offsets[goes[k]]},
            device_id_type=MESH,
        )

    for_each(range(slots), lambda k: goes[k], lambda k: trace_copy(k).start())

    for i in (FLUX, NBR, ROT, LIFT, ORIENT, CLUS):
        loads[i].wait()

    def flux_side(j, side, values, finish):
        lanes = pl.ds(pl.multiple_of(j * E, E), E)
        x = [values[q * FP : (q + 1) * FP, lanes] for q in range(Q)]
        for p in range(Q):
            total = None
            for q in range(Q):
                term = flux_ref[j, p, q, side : side + 1, :] * x[q]
                total = term if total is None else total + term
            finish(j, p, total)

    def own_step(j, carry):
        def finish(j, p, total):
            ft[pl.ds(pl.multiple_of(j * FP, FP), FP), p * E : (p + 1) * E] = total

        flux_side(j, 0, pool, finish)
        return carry

    lax.fori_loop(0, NF, own_step, 0)

    build[...] = jnp.zeros_like(build)
    for d in range(3):
        high, low = halves(stiff_ref[d].T)
        build[d * B : (d + 1) * B, 0:B] = high
        build[d * B : (d + 1) * B, BP : BP + B] = high
        build[d * B : (d + 1) * B, 2 * BP : 2 * BP + B] = low
    wv[...] = build[0 : 3 * B, 0 : 3 * BP].astype(BF16)
    multiply(wv)

    def volume_step(block, carry):
        def finish(p, total):
            base[p] = adj_ref[0, p] + total

        contract(block, finish)
        return carry

    lax.fori_loop(0, 3, volume_step, 0)

    for j in range(NF):
        row = lax.broadcasted_iota(jnp.int32, (FACES + slots * cap, E), 0)
        hit = row == nbr_ref[j : j + 1, :]
        oh[:, j * E : (j + 1) * E] = jnp.where(hit, 1.0, 0.0).astype(BF16)
    gath[...] = nn_dot(pcat[:, 0:FACES], oh[0:FACES, :]) + nn_dot(pcat[:, FACES : 2 * FACES], oh[0:FACES, :])

    build[...] = jnp.zeros_like(build)
    for o in range(3):
        high, low = halves(rot_ref[o])
        for i in range(3):
            rows = slice(i * 72 + o * FP, i * 72 + o * FP + F)
            build[rows, i * 72 : i * 72 + F] = high
            build[rows, i * 72 + FP : i * 72 + FP + F] = high
            build[rows, i * 72 + 2 * FP : i * 72 + 2 * FP + F] = low
    rb[...] = build[0:QP, 0:ROWS].astype(BF16)
    build[...] = jnp.zeros_like(build)
    for j in range(NF):
        high, low = halves(lift_ref[:, j, :].T)
        build[0:B, j * FP : j * FP + F] = high
        build[0:B, NF * FP + j * FP : NF * FP + j * FP + F] = high
        build[B : 2 * B, j * FP : j * FP + F] = low
    lw[...] = build[0 : 2 * B, 0 : 2 * NF * FP].astype(BF16)

    def no_faces(k):
        recvbuf[k * cap : (k + 1) * cap] = jnp.zeros((cap, ROWS), F32)

    for_each(range(slots), lambda k: comes[k], lambda k: trace_copy(k).wait_recv())
    for k in range(slots):

        @pl.when(jnp.logical_not(present[comes[k]]))
        def _():
            no_faces(k)

    high, low = halves(recvbuf[...].T)
    far = oh[FACES : FACES + slots * cap, :]
    gath[...] = gath[...] + nn_dot(high.astype(BF16), far) + nn_dot(low.astype(BF16), far)

    xg[QP:ROWS, :] = jnp.zeros((ROWS - QP, FACES), F32)
    for t in range(3):
        for i in range(3):
            q = 3 * t + i
            high, low = halves(gath[q * FP : (q + 1) * FP, :])
            xg[i * 72 : i * 72 + FP, :] = high
            xg[i * 72 + FP : i * 72 + 2 * FP, :] = low
            xg[i * 72 + 2 * FP : i * 72 + 3 * FP, :] = high
        result = nn_dot(rb[...], xg[...].astype(BF16))
        for i in range(3):
            q = 3 * t + i
            for j in range(NF):
                o = orient_ref[j : j + 1, :]
                r = [
                    result[i * 72 + n * FP : i * 72 + (n + 1) * FP, j * E : (j + 1) * E] for n in range(3)
                ]
                turned[q * FP : (q + 1) * FP, j * E : (j + 1) * E] = jnp.where(
                    o == 0, r[0], jnp.where(o == 1, r[1], r[2])
                )

    def far_step(j, carry):
        def finish(j, p, total):
            rows = pl.ds(pl.multiple_of(j * FP, FP), FP)
            lanes = slice(p * E, (p + 1) * E)
            ft[rows, lanes] = ft[rows, lanes] + total

        flux_side(j, 1, turned, finish)
        return carry

    lax.fori_loop(0, NF, far_step, 0)

    high, low = halves(ft[...])
    ftb[0 : NF * FP, :] = high.astype(BF16)
    ftb[NF * FP : 2 * NF * FP, :] = low.astype(BF16)
    moves = clus_ref[...] == 0
    for tile in range(5):
        wide = min(2, Q - 2 * tile)
        result = nn_dot(lw[...], ftb[:, tile * 256 : tile * 256 + wide * E])
        surface = result[0:B] + result[B : 2 * B]
        for i in range(wide):
            p = 2 * tile + i
            out_ref[0, p] = jnp.where(moves, base[p] - surface[:, i * E : (i + 1) * E], adj_ref[0, p])

    def no_window(n):
        recvwin[n] = jnp.zeros((8, E), F32)

    for_each(count, lambda n: 2 * reach - windows[n][0], lambda n: window_copy(n).wait_recv())
    for o in range(2 * reach + 1):

        @pl.when(jnp.logical_not(present[2 * reach - o]))
        def _():
            for n in count:
                if windows[n][0] == o:
                    no_window(n)

    total = sendwin[reach]
    for n in count:
        total = total + recvwin[n]
    grad_ref[...] = total[0:PARAMS]

    for_each(range(slots), lambda k: goes[k], lambda k: trace_copy(k).wait_send())
    for_each(count, lambda n: windows[n][0], lambda n: window_copy(n).wait_send())


def store(next_ref, sums_ref, out_ref, grad_ref, sem):
    copies = [
        pltpu.make_async_copy(next_ref, out_ref, sem.at[0]),
        pltpu.make_async_copy(sums_ref, grad_ref, sem.at[1]),
    ]
    for copy in copies:
        copy.start()
    for copy in copies:
        copy.wait()


def solution(mesh):
    n_dom, n_src = mesh.shape["dom"], mesh.shape["src"]

    def body(adj, fwd, star, flux, stiff, restr, rot, lift, kw, nbr, send, orient, clus, cell):
        reach, cap = send.shape[0] // 2, send.shape[1]
        star = star.transpose(1, 2, 0, 3)
        flux = flux.transpose(0, 2, 3, 1, 4)
        restr = restr.transpose(2, 0, 1)
        lift = lift.transpose(1, 0, 2)
        kw = kw.transpose(1, 0, 2)
        slots = 2 * reach
        others = (slots + 1) * n_src - 1
        operands = (
            adj, fwd, star, flux, stiff, restr, rot, lift, kw, nbr, send, orient,
            clus.reshape(1, E), cell.reshape(1, E),
        )
        vmem = pl.BlockSpec(memory_space=pltpu.VMEM)
        dma = pltpu.SemaphoreType.DMA
        operands = tuple(pltpu.with_memory_space_constraint(x, pltpu.HBM) for x in operands)
        results = pl.pallas_call(
            functools.partial(kernel, n_dom, n_src, reach, cap),
            out_shape=(
                pltpu.VMEM(adj.shape, F32),
                pltpu.VMEM((PARAMS, E), F32),
            ),
            in_specs=[pl.BlockSpec(memory_space=pltpu.HBM)] * 14,
            out_specs=(vmem, vmem),
            scratch_shapes=[
                *[(pltpu.SMEM if i == KW else pltpu.VMEM)(x.shape, x.dtype) for i, x in enumerate(operands)],
                pltpu.VMEM((ROWS, 256), F32),
                pltpu.VMEM((3 * B, 3 * BP), BF16),
                pltpu.VMEM((3 * B, 3 * BP), BF16),
                pltpu.VMEM((NF * FP, 3 * BP), BF16),
                pltpu.VMEM((QP, ROWS), BF16),
                pltpu.VMEM((2 * B, 2 * NF * FP), BF16),
                pltpu.VMEM((3 * BP, Q * E), BF16),
                pltpu.VMEM((3 * B, Q * E), F32),
                pltpu.VMEM((Q, B, E), F32),
                pltpu.VMEM((Q, B, E), F32),
                pltpu.VMEM((ROWS, FACES), F32),
                pltpu.VMEM((ROWS, 2 * FACES), BF16),
                pltpu.VMEM((FACES + slots * cap, FACES), BF16),
                pltpu.VMEM((slots * cap, FACES), BF16),
                pltpu.VMEM((ROWS, FACES), F32),
                pltpu.VMEM((ROWS, FACES), F32),
                pltpu.VMEM((QP, FACES), F32),
                pltpu.VMEM((NF * FP, Q * E), F32),
                pltpu.VMEM((2 * NF * FP, Q * E), BF16),
                pltpu.VMEM((Q, B, E), F32),
                pltpu.VMEM((slots * cap, ROWS), F32),
                pltpu.VMEM((slots * cap, ROWS), F32),
                pltpu.VMEM((slots + 1, 8, E), F32),
                pltpu.VMEM((others, 8, E), F32),
                dma((14,)),
                dma((slots,)),
                dma((slots,)),
                dma((others,)),
                dma((others,)),
            ],
            compiler_params=pltpu.CompilerParams(
                collective_id=0, has_side_effects=True, vmem_limit_bytes=32 * 1024 * 1024
            ),
        )(*operands)
        return pl.pallas_call(
            store,
            out_shape=(
                jax.ShapeDtypeStruct(adj.shape, F32),
                jax.ShapeDtypeStruct((PARAMS, E), F32),
            ),
            in_specs=[vmem, vmem],
            out_specs=[pl.BlockSpec(memory_space=pltpu.HBM)] * 2,
            scratch_shapes=[dma((2,))],
            compiler_params=pltpu.CompilerParams(vmem_limit_bytes=1024 * 1024),
        )(*(pltpu.with_memory_space_constraint(x, pltpu.VMEM) for x in results))

    placed = (
        P("src", None, None, "dom"),
        P("src", None, None, "dom"),
        P(None, None, None, "dom"),
        P(None, None, None, None, "dom"),
        P(),
        P(),
        P(),
        P(),
        P(),
        P(None, "dom"),
        P(None, "dom"),
        P(None, "dom"),
        P("dom"),
        P("dom"),
    )
    return jax.shard_map(
        body,
        mesh=mesh,
        in_specs=placed,
        out_specs=(P("src", None, None, "dom"), P(None, "dom")),
        check_vma=False,
    )
```

```python
import functools

import jax
import jax.numpy as jnp
from jax import lax
from jax.experimental import pallas as pl
from jax.experimental.pallas import tpu as pltpu
from jax.sharding import PartitionSpec as P

MESH = pl.DeviceIdType.MESH
F32 = jnp.float32
BF16 = jnp.bfloat16

Q = 9
B = 56
BP = 64
F = 21
FP = 24
E = 128
NF = 4
FACES = NF * E
ROWS = 224
QP = Q * FP
PARAMS = 3

ADJ, FWD, STAR, FLUX, STIFF, RESTR, ROT, LIFT, KW, NBR, SEND, ORIENT, CLUS, CELL = range(14)


def halves(x):
    high = x.astype(BF16).astype(F32)
    return high, x - high


def nt_dot(a, b):
    return lax.dot_general(a, b, (((1,), (1,)), ((), ())), preferred_element_type=F32)


def nn_dot(a, b):
    return jnp.dot(a, b, preferred_element_type=F32)


def kernel(
    n_dom,
    n_src,
    reach,
    cap,
    *refs,
):
    inputs, (out_ref, grad_ref), refs = refs[:14], refs[14:16], refs[16:]
    held, refs = refs[:14], refs[14:]
    (
        adj_ref, fwd_ref, star_ref, flux_ref, stiff_ref, restr_ref, rot_ref, lift_ref, kw_ref,
        nbr_ref, send_ref, orient_ref, clus_ref, cell_ref,
    ) = held
    (
    build,
    wk,
    wv,
    wt,
    rb,
    lw,
    v3,
    even,
    odd,
    integral,
    fwd32,
    pool,
    pcat,
    oh,
    ohs,
    gath,
    xg,
    turned,
    ft,
    ftb,
    base,
    sendbuf,
    recvbuf,
    sendwin,
    recvwin,
    load_sem,
    send_sem,
    recv_sem,
    wsend_sem,
    wrecv_sem,
    ) = refs
    dom = lax.axis_index("dom")
    src = lax.axis_index("src")
    slots = 2 * reach
    offsets = [o - reach for o in range(2 * reach + 1)]
    present = [(dom + d >= 0) & (dom + d < n_dom) for d in offsets]
    sources = [lax.rem(src + s, n_src) for s in range(n_src)]
    goes = [reach + k + 1 for k in range(reach)] + [reach - k - 1 for k in range(reach)]
    comes = [2 * reach - o for o in goes]
    windows = [(o, s) for o in range(2 * reach + 1) for s in range(n_src) if (o, s) != (reach, 0)]

    def for_each(keys, where, action):
        for o in range(2 * reach + 1):
            mine = [k for k in keys if where(k) == o]
            if not mine:
                continue

            @pl.when(present[o])
            def _():
                for k in mine:
                    action(k)

    loads = [pltpu.make_async_copy(inputs[i], held[i], load_sem.at[i]) for i in range(14)]
    for i in (STIFF, RESTR, SEND, ADJ, STAR, FWD, KW, CELL, FLUX, NBR, ROT, LIFT, ORIENT, CLUS):
        loads[i].start()

    barrier = pltpu.get_barrier_semaphore()

    def greet(key):
        o, s = key
        pl.semaphore_signal(
            barrier, inc=1, device_id={"dom": dom + offsets[o], "src": sources[s]}, device_id_type=MESH
        )

    for_each(windows, lambda key: key[0], greet)

    build[...] = jnp.zeros_like(build)
    loads[STIFF].wait()
    for d in range(3):
        high, low = halves(stiff_ref[d])
        build[d * B : (d + 1) * B, 0:B] = high
        build[d * B : (d + 1) * B, BP : BP + B] = high
        build[d * B : (d + 1) * B, 2 * BP : 2 * BP + B] = low
    wk[...] = build[0 : 3 * B, 0 : 3 * BP].astype(BF16)

    loads[RESTR].wait()
    build[...] = jnp.zeros_like(build)
    for j in range(NF):
        high, low = halves(restr_ref[:, j, :])
        build[j * FP : j * FP + F, 0:B] = high
        build[j * FP : j * FP + F, BP : BP + B] = high
        build[j * FP : j * FP + F, 2 * BP : 2 * BP + B] = low
    wt[...] = build[0 : NF * FP, 0 : 3 * BP].astype(BF16)
    loads[SEND].wait()
    listed = send_ref[...].astype(F32).T
    face_lane = lax.broadcasted_iota(jnp.int32, (cap, FACES), 1).astype(F32)
    for k in range(slots):
        hit = listed[:, k : k + 1] == face_lane
        ohs[k * cap : (k + 1) * cap, :] = jnp.where(hit, 1.0, 0.0).astype(BF16)

    zeros8 = jnp.zeros((BP - B, E), F32)

    def put_state(q, value):
        high, low = halves(jnp.concatenate([value, zeros8], axis=0))
        lanes = pl.ds(pl.multiple_of(q * E, E), E)
        v3[0:BP, lanes] = high.astype(BF16)
        v3[BP : 2 * BP, lanes] = low.astype(BF16)
        v3[2 * BP : 3 * BP, lanes] = high.astype(BF16)

    def start_state(q, carry):
        value = adj_ref[0, q]
        integral[q] = value
        put_state(q, value)
        return carry

    loads[ADJ].wait()
    lax.fori_loop(0, Q, start_state, 0)
    loads[STAR].wait()

    def multiply(weights, group, target):
        lanes = pl.ds(pl.multiple_of(group * 3 * E, E), 3 * E)
        target[group] = nn_dot(weights[...], v3[:, lanes])

    def contract(block, source, finish):
        totals = [None] * 3
        for q in range(Q):
            for d in range(3):
                a = source[q // 3, d * B : (d + 1) * B, (q % 3) * E : (q % 3 + 1) * E]
                for i in range(3):
                    term = star_ref[3 * block + i, q, d : d + 1, :] * a
                    totals[i] = term if totals[i] is None else totals[i] + term
        for i in range(3):
            finish(3 * block + i, totals[i])

    def degree_step(scale, now, later):
        def finish(p, total):
            value = total * scale
            integral[p] = integral[p] + value
            put_state(p, integral[p] if later is None else value)

        multiply(wk, 2, now)
        contract(0, now, finish)

        def block_step(block, c):
            if later is not None:
                multiply(wk, block - 1, later)
            contract(block, now, finish)
            return c

        lax.fori_loop(1, 3, block_step, 0)

    multiply(wk, 0, even)
    multiply(wk, 1, even)

    def two_degrees(k, carry):
        degree_step(jnp.where(k == 0, jnp.float32(-1 / 2), jnp.float32(-1 / 4)), even, odd)
        degree_step(jnp.where(k == 0, jnp.float32(-1 / 3), jnp.float32(-1 / 5)), odd, even)
        return carry

    lax.fori_loop(0, 2, two_degrees, 0)
    degree_step(jnp.float32(-1 / 6), even, None)

    for i in (FWD, KW, CELL):
        loads[i].wait()
    fwd32[...] = fwd_ref[0].astype(F32)

    def pair_step(q, carry):
        own = integral[q]
        sums = list(carry)
        for r in range(Q):
            product = own * fwd32[r]
            pair = product[0:8]
            for c in range(1, 7):
                pair = pair + product[8 * c : 8 * c + 8]
            for n in range(PARAMS):
                sums[n] = sums[n] + kw_ref[q, n, r] * pair
        return tuple(sums)

    sums = lax.fori_loop(0, Q, pair_step, tuple(jnp.zeros((8, E), F32) for _ in range(PARAMS)))
    terms = jnp.concatenate(
        [jnp.sum(s, axis=0, keepdims=True) for s in sums] + [jnp.zeros((8 - PARAMS, E), F32)], axis=0
    )
    high, low = halves(terms)
    both = jnp.concatenate([high, low], axis=0).astype(BF16)
    place = cell_ref[...] - (dom - reach) * E
    for o in range(2 * reach + 1):
        row = lax.broadcasted_iota(jnp.int32, (E, E), 0) + o * E
        hit = jnp.where(row == place, 1.0, 0.0).astype(BF16)
        summed = nt_dot(both, hit)
        sendwin[o] = (summed[0:8] + summed[8:16])[0:PARAMS]

    neighbours = -1
    for here in present:
        neighbours = neighbours + n_src * here.astype(jnp.int32)
    pl.semaphore_wait(barrier, neighbours)

    def window_copy(n):
        o, s = windows[n]
        return pltpu.make_async_remote_copy(
            src_ref=sendwin.at[o],
            dst_ref=recvwin.at[n],
            send_sem=wsend_sem.at[n],
            recv_sem=wrecv_sem.at[n],
            device_id={"dom": dom + offsets[o], "src": sources[s]},
            device_id_type=MESH,
        )

    count = range(len(windows))
    for_each(count, lambda n: windows[n][0], lambda n: window_copy(n).start())

    pool[QP:ROWS, :] = jnp.zeros((ROWS - QP, FACES), F32)
    for tile in range(5):
        wide = min(2, Q - 2 * tile)
        result = nn_dot(wt[...], v3[:, tile * 256 : tile * 256 + wide * E])
        for i in range(wide):
            q = 2 * tile + i
            for j in range(NF):
                pool[q * FP : (q + 1) * FP, j * E : (j + 1) * E] = result[
                    j * FP : (j + 1) * FP, i * E : (i + 1) * E
                ]
    high, low = halves(pool[...])
    pcat[:, 0:FACES] = high.astype(BF16)
    pcat[:, FACES : 2 * FACES] = low.astype(BF16)

    sendbuf[...] = nt_dot(ohs[...], pcat[:, 0:FACES]) + nt_dot(ohs[...], pcat[:, FACES : 2 * FACES])

    def trace_copy(k):
        part = pl.ds(k * cap, cap)
        return pltpu.make_async_remote_copy(
            src_ref=sendbuf.at[part],
            dst_ref=recvbuf.at[part],
            send_sem=send_sem.at[k],
            recv_sem=recv_sem.at[k],
            device_id={"dom": dom + offsets[goes[k]]},
            device_id_type=MESH,
        )

    for_each(range(slots), lambda k: goes[k], lambda k: trace_copy(k).start())

    for i in (FLUX, NBR, ROT, LIFT, ORIENT, CLUS):
        loads[i].wait()

    def flux_side(j, side, values, finish):
        lanes = pl.ds(pl.multiple_of(j * E, E), E)
        x = [values[q * FP : (q + 1) * FP, lanes] for q in range(Q)]
        for p in range(Q):
            total = None
            for q in range(Q):
                term = flux_ref[j, p, q, side : side + 1, :] * x[q]
                total = term if total is None else total + term
            finish(j, p, total)

    def own_step(j, carry):
        def finish(j, p, total):
            ft[pl.ds(pl.multiple_of(j * FP, FP), FP), p * E : (p + 1) * E] = total

        flux_side(j, 0, pool, finish)
        return carry

    lax.fori_loop(0, NF, own_step, 0)

    build[...] = jnp.zeros_like(build)
    for d in range(3):
        high, low = halves(stiff_ref[d].T)
        build[d * B : (d + 1) * B, 0:B] = high
        build[d * B : (d + 1) * B, BP : BP + B] = high
        build[d * B : (d + 1) * B, 2 * BP : 2 * BP + B] = low
    wv[...] = build[0 : 3 * B, 0 : 3 * BP].astype(BF16)
    for group in range(3):
        multiply(wv, group, odd)

    def volume_step(block, carry):
        def finish(p, total):
            base[p] = adj_ref[0, p] + total

        contract(block, odd, finish)
        return carry

    lax.fori_loop(0, 3, volume_step, 0)

    for j in range(NF):
        row = lax.broadcasted_iota(jnp.int32, (FACES + slots * cap, E), 0)
        hit = row == nbr_ref[j : j + 1, :]
        oh[:, j * E : (j + 1) * E] = jnp.where(hit, 1.0, 0.0).astype(BF16)
    gath[...] = nn_dot(pcat[:, 0:FACES], oh[0:FACES, :]) + nn_dot(pcat[:, FACES : 2 * FACES], oh[0:FACES, :])

    build[...] = jnp.zeros_like(build)
    for o in range(3):
        high, low = halves(rot_ref[o])
        for i in range(3):
            rows = slice(i * 72 + o * FP, i * 72 + o * FP + F)
            build[rows, i * 72 : i * 72 + F] = high
            build[rows, i * 72 + FP : i * 72 + FP + F] = high
            build[rows, i * 72 + 2 * FP : i * 72 + 2 * FP + F] = low
    rb[...] = build[0:QP, 0:ROWS].astype(BF16)
    build[...] = jnp.zeros_like(build)
    for j in range(NF):
        high, low = halves(lift_ref[:, j, :].T)
        build[0:B, j * FP : j * FP + F] = high
        build[0:B, NF * FP + j * FP : NF * FP + j * FP + F] = high
        build[B : 2 * B, j * FP : j * FP + F] = low
    lw[...] = build[0 : 2 * B, 0 : 2 * NF * FP].astype(BF16)

    def no_faces(k):
        recvbuf[k * cap : (k + 1) * cap] = jnp.zeros((cap, ROWS), F32)

    for_each(range(slots), lambda k: comes[k], lambda k: trace_copy(k).wait_recv())
    for k in range(slots):

        @pl.when(jnp.logical_not(present[comes[k]]))
        def _():
            no_faces(k)

    high, low = halves(recvbuf[...].T)
    far = oh[FACES : FACES + slots * cap, :]
    gath[...] = gath[...] + nn_dot(high.astype(BF16), far) + nn_dot(low.astype(BF16), far)

    xg[QP:ROWS, :] = jnp.zeros((ROWS - QP, FACES), F32)
    for t in range(3):
        for i in range(3):
            q = 3 * t + i
            high, low = halves(gath[q * FP : (q + 1) * FP, :])
            xg[i * 72 : i * 72 + FP, :] = high
            xg[i * 72 + FP : i * 72 + 2 * FP, :] = low
            xg[i * 72 + 2 * FP : i * 72 + 3 * FP, :] = high
        result = nn_dot(rb[...], xg[...].astype(BF16))
        for i in range(3):
            q = 3 * t + i
            for j in range(NF):
                o = orient_ref[j : j + 1, :]
                r = [
                    result[i * 72 + n * FP : i * 72 + (n + 1) * FP, j * E : (j + 1) * E] for n in range(3)
                ]
                turned[q * FP : (q + 1) * FP, j * E : (j + 1) * E] = jnp.where(
                    o == 0, r[0], jnp.where(o == 1, r[1], r[2])
                )

    def far_step(j, carry):
        def finish(j, p, total):
            rows = pl.ds(pl.multiple_of(j * FP, FP), FP)
            lanes = slice(p * E, (p + 1) * E)
            ft[rows, lanes] = ft[rows, lanes] + total

        flux_side(j, 1, turned, finish)
        return carry

    lax.fori_loop(0, NF, far_step, 0)

    high, low = halves(ft[...])
    ftb[0 : NF * FP, :] = high.astype(BF16)
    ftb[NF * FP : 2 * NF * FP, :] = low.astype(BF16)
    moves = clus_ref[...] == 0
    for tile in range(5):
        wide = min(2, Q - 2 * tile)
        result = nn_dot(lw[...], ftb[:, tile * 256 : tile * 256 + wide * E])
        surface = result[0:B] + result[B : 2 * B]
        for i in range(wide):
            p = 2 * tile + i
            out_ref[0, p] = jnp.where(moves, base[p] - surface[:, i * E : (i + 1) * E], adj_ref[0, p])

    def no_window(n):
        recvwin[n] = jnp.zeros((PARAMS, E), F32)

    for_each(count, lambda n: 2 * reach - windows[n][0], lambda n: window_copy(n).wait_recv())
    for o in range(2 * reach + 1):

        @pl.when(jnp.logical_not(present[2 * reach - o]))
        def _():
            for n in count:
                if windows[n][0] == o:
                    no_window(n)

    total = sendwin[reach]
    for n in count:
        total = total + recvwin[n]
    grad_ref[...] = total

    for_each(range(slots), lambda k: goes[k], lambda k: trace_copy(k).wait_send())
    for_each(count, lambda n: windows[n][0], lambda n: window_copy(n).wait_send())


def store(next_ref, sums_ref, out_ref, grad_ref, sem):
    copies = [
        pltpu.make_async_copy(next_ref, out_ref, sem.at[0]),
        pltpu.make_async_copy(sums_ref, grad_ref, sem.at[1]),
    ]
    for copy in copies:
        copy.start()
    for copy in copies:
        copy.wait()


def solution(mesh):
    n_dom, n_src = mesh.shape["dom"], mesh.shape["src"]

    def body(adj, fwd, star, flux, stiff, restr, rot, lift, kw, nbr, send, orient, clus, cell):
        reach, cap = send.shape[0] // 2, send.shape[1]
        star = star.transpose(1, 2, 0, 3)
        flux = flux.transpose(0, 2, 3, 1, 4)
        restr = restr.transpose(2, 0, 1)
        lift = lift.transpose(1, 0, 2)
        kw = kw.transpose(1, 0, 2)
        slots = 2 * reach
        others = (slots + 1) * n_src - 1
        operands = (
            adj, fwd, star, flux, stiff, restr, rot, lift, kw, nbr, send, orient,
            clus.reshape(1, E), cell.reshape(1, E),
        )
        vmem = pl.BlockSpec(memory_space=pltpu.VMEM)
        dma = pltpu.SemaphoreType.DMA
        operands = tuple(pltpu.with_memory_space_constraint(x, pltpu.HBM) for x in operands)
        results = pl.pallas_call(
            functools.partial(kernel, n_dom, n_src, reach, cap),
            out_shape=(
                pltpu.VMEM(adj.shape, F32),
                pltpu.VMEM((PARAMS, E), F32),
            ),
            in_specs=[pl.BlockSpec(memory_space=pltpu.HBM)] * 14,
            out_specs=(vmem, vmem),
            scratch_shapes=[
                *[(pltpu.SMEM if i == KW else pltpu.VMEM)(x.shape, x.dtype) for i, x in enumerate(operands)],
                pltpu.VMEM((ROWS, 256), F32),
                pltpu.VMEM((3 * B, 3 * BP), BF16),
                pltpu.VMEM((3 * B, 3 * BP), BF16),
                pltpu.VMEM((NF * FP, 3 * BP), BF16),
                pltpu.VMEM((QP, ROWS), BF16),
                pltpu.VMEM((2 * B, 2 * NF * FP), BF16),
                pltpu.VMEM((3 * BP, Q * E), BF16),
                pltpu.VMEM((3, 3 * B, 3 * E), F32),
                pltpu.VMEM((3, 3 * B, 3 * E), F32),
                pltpu.VMEM((Q, B, E), F32),
                pltpu.VMEM((Q, B, E), F32),
                pltpu.VMEM((ROWS, FACES), F32),
                pltpu.VMEM((ROWS, 2 * FACES), BF16),
                pltpu.VMEM((FACES + slots * cap, FACES), BF16),
                pltpu.VMEM((slots * cap, FACES), BF16),
                pltpu.VMEM((ROWS, FACES), F32),
                pltpu.VMEM((ROWS, FACES), F32),
                pltpu.VMEM((QP, FACES), F32),
                pltpu.VMEM((NF * FP, Q * E), F32),
                pltpu.VMEM((2 * NF * FP, Q * E), BF16),
                pltpu.VMEM((Q, B, E), F32),
                pltpu.VMEM((slots * cap, ROWS), F32),
                pltpu.VMEM((slots * cap, ROWS), F32),
                pltpu.VMEM((slots + 1, PARAMS, E), F32),
                pltpu.VMEM((others, PARAMS, E), F32),
                dma((14,)),
                dma((slots,)),
                dma((slots,)),
                dma((others,)),
                dma((others,)),
            ],
            compiler_params=pltpu.CompilerParams(
                collective_id=0, has_side_effects=True, vmem_limit_bytes=32 * 1024 * 1024
            ),
        )(*operands)
        return pl.pallas_call(
            store,
            out_shape=(
                jax.ShapeDtypeStruct(adj.shape, F32),
                jax.ShapeDtypeStruct((PARAMS, E), F32),
            ),
            in_specs=[vmem, vmem],
            out_specs=[pl.BlockSpec(memory_space=pltpu.HBM)] * 2,
            scratch_shapes=[dma((2,))],
            compiler_params=pltpu.CompilerParams(vmem_limit_bytes=1024 * 1024),
        )(*(pltpu.with_memory_space_constraint(x, pltpu.VMEM) for x in results))

    placed = (
        P("src", None, None, "dom"),
        P("src", None, None, "dom"),
        P(None, None, None, "dom"),
        P(None, None, None, None, "dom"),
        P(),
        P(),
        P(),
        P(),
        P(),
        P(None, "dom"),
        P(None, "dom"),
        P(None, "dom"),
        P("dom"),
        P("dom"),
    )
    return jax.shard_map(
        body,
        mesh=mesh,
        in_specs=placed,
        out_specs=(P("src", None, None, "dom"), P(None, "dom")),
        check_vma=False,
    )
```

```python
import functools

import jax
import jax.numpy as jnp
from jax import lax
from jax.experimental import pallas as pl
from jax.experimental.pallas import tpu as pltpu
from jax.sharding import PartitionSpec as P

MESH = pl.DeviceIdType.MESH
F32 = jnp.float32
BF16 = jnp.bfloat16

Q = 9
B = 56
BP = 64
F = 21
FP = 24
E = 128
NF = 4
FACES = NF * E
ROWS = 224
QP = Q * FP
PARAMS = 3

ADJ, FWD, STAR, FLUX, STIFF, RESTR, ROT, LIFT, KW, NBR, SEND, ORIENT, CLUS, CELL = range(14)


def halves(x):
    high = x.astype(BF16).astype(F32)
    return high, x - high


def nt_dot(a, b):
    return lax.dot_general(a, b, (((1,), (1,)), ((), ())), preferred_element_type=F32)


def nn_dot(a, b):
    return jnp.dot(a, b, preferred_element_type=F32)


def kernel(
    n_dom,
    n_src,
    reach,
    cap,
    *refs,
):
    inputs, (out_ref, grad_ref), refs = refs[:14], refs[14:16], refs[16:]
    held, refs = refs[:14], refs[14:]
    (
        adj_ref, fwd_ref, star_ref, flux_ref, stiff_ref, restr_ref, rot_ref, lift_ref, kw_ref,
        nbr_ref, send_ref, orient_ref, clus_ref, cell_ref,
    ) = held
    (
    build,
    wk,
    wv,
    wt,
    rb,
    lw,
    v3,
    even,
    odd,
    integral,
    fwd32,
    pool,
    pcat,
    oh,
    ohs,
    ohc,
    gath,
    xg,
    turned,
    ft,
    ftb,
    base,
    sendbuf,
    recvbuf,
    sendwin,
    recvwin,
    load_sem,
    send_sem,
    recv_sem,
    wsend_sem,
    wrecv_sem,
    ) = refs
    dom = lax.axis_index("dom")
    src = lax.axis_index("src")
    slots = 2 * reach
    offsets = [o - reach for o in range(2 * reach + 1)]
    present = [(dom + d >= 0) & (dom + d < n_dom) for d in offsets]
    sources = [lax.rem(src + s, n_src) for s in range(n_src)]
    goes = [reach + k + 1 for k in range(reach)] + [reach - k - 1 for k in range(reach)]
    comes = [2 * reach - o for o in goes]
    windows = [(o, s) for o in range(2 * reach + 1) for s in range(n_src) if (o, s) != (reach, 0)]

    def for_each(keys, where, action):
        for o in reversed(range(2 * reach + 1)):
            mine = [k for k in keys if where(k) == o]
            if not mine:
                continue

            @pl.when(present[o])
            def _():
                for k in mine:
                    action(k)

    loads = [pltpu.make_async_copy(inputs[i], held[i], load_sem.at[i]) for i in range(14)]
    for i in (STIFF, ADJ, STAR, RESTR, SEND, CELL):
        loads[i].start()

    barrier = pltpu.get_barrier_semaphore()

    def greet(key):
        o, s = key
        pl.semaphore_signal(
            barrier, inc=1, device_id={"dom": dom + offsets[o], "src": sources[s]}, device_id_type=MESH
        )

    for_each(windows, lambda key: key[0], greet)

    build[...] = jnp.zeros_like(build)
    loads[STIFF].wait()
    for d in range(3):
        high, low = halves(stiff_ref[d])
        build[d * B : (d + 1) * B, 0:B] = high
        build[d * B : (d + 1) * B, BP : BP + B] = high
        build[d * B : (d + 1) * B, 2 * BP : 2 * BP + B] = low
    wk[...] = build[0 : 3 * B, 0 : 3 * BP].astype(BF16)

    loads[RESTR].wait()
    build[...] = jnp.zeros_like(build)
    for j in range(NF):
        high, low = halves(restr_ref[:, j, :])
        build[j * FP : j * FP + F, 0:B] = high
        build[j * FP : j * FP + F, BP : BP + B] = high
        build[j * FP : j * FP + F, 2 * BP : 2 * BP + B] = low
    wt[...] = build[0 : NF * FP, 0 : 3 * BP].astype(BF16)
    loads[SEND].wait()
    listed = send_ref[...].astype(F32).T
    face_lane = lax.broadcasted_iota(jnp.int32, (cap, FACES), 1).astype(F32)
    for k in range(slots):
        hit = listed[:, k : k + 1] == face_lane
        ohs[k * cap : (k + 1) * cap, :] = jnp.where(hit, 1.0, 0.0).astype(BF16)
    loads[CELL].wait()
    place = cell_ref[...] - (dom - reach) * E
    row = lax.broadcasted_iota(jnp.int32, ((2 * reach + 1) * E, E), 0)
    ohc[...] = jnp.where(row == place, 1.0, 0.0).astype(BF16)

    zeros8 = jnp.zeros((BP - B, E), F32)

    def put_state(q, value):
        high, low = halves(jnp.concatenate([value, zeros8], axis=0))
        lanes = pl.ds(pl.multiple_of(q * E, E), E)
        v3[0:BP, lanes] = high.astype(BF16)
        v3[BP : 2 * BP, lanes] = low.astype(BF16)
        v3[2 * BP : 3 * BP, lanes] = high.astype(BF16)

    def start_state(q, carry):
        value = adj_ref[0, q]
        integral[q] = value
        put_state(q, value)
        return carry

    loads[ADJ].wait()
    lax.fori_loop(0, Q, start_state, 0)
    loads[STAR].wait()
    for i in (FWD, KW, FLUX, NBR, ROT, LIFT, ORIENT, CLUS):
        loads[i].start()

    def multiply(weights, group, target):
        lanes = pl.ds(pl.multiple_of(group * 3 * E, E), 3 * E)
        target[group] = nn_dot(weights[...], v3[:, lanes])

    def contract(block, source, finish):
        totals = [None] * 3
        for q in range(Q):
            for d in range(3):
                a = source[q // 3, d * B : (d + 1) * B, (q % 3) * E : (q % 3 + 1) * E]
                for i in range(3):
                    term = star_ref[3 * block + i, q, d : d + 1, :] * a
                    totals[i] = term if totals[i] is None else totals[i] + term
        for i in range(3):
            finish(3 * block + i, totals[i])

    def degree_step(scale, now, later):
        def finish(p, total):
            value = total * scale
            integral[p] = integral[p] + value
            put_state(p, integral[p] if later is None else value)

        multiply(wk, 2, now)
        contract(0, now, finish)

        def block_step(block, c):
            if later is not None:
                multiply(wk, block - 1, later)
            contract(block, now, finish)
            return c

        lax.fori_loop(1, 3, block_step, 0)

    multiply(wk, 0, even)
    multiply(wk, 1, even)

    def two_degrees(k, carry):
        degree_step(jnp.where(k == 0, jnp.float32(-1 / 2), jnp.float32(-1 / 4)), even, odd)
        degree_step(jnp.where(k == 0, jnp.float32(-1 / 3), jnp.float32(-1 / 5)), odd, even)
        return carry

    lax.fori_loop(0, 2, two_degrees, 0)
    degree_step(jnp.float32(-1 / 6), even, None)

    for i in (FWD, KW):
        loads[i].wait()
    fwd32[...] = fwd_ref[0].astype(F32)

    def pair_step(q, carry):
        own = integral[q]
        sums = list(carry)
        for r in range(Q):
            product = own * fwd32[r]
            pair = product[0:8]
            for c in range(1, 7):
                pair = pair + product[8 * c : 8 * c + 8]
            for n in range(PARAMS):
                sums[n] = sums[n] + kw_ref[q, n, r] * pair
        return tuple(sums)

    sums = lax.fori_loop(0, Q, pair_step, tuple(jnp.zeros((8, E), F32) for _ in range(PARAMS)))
    terms = jnp.concatenate(
        [jnp.sum(s, axis=0, keepdims=True) for s in sums] + [jnp.zeros((8 - PARAMS, E), F32)], axis=0
    )
    high, low = halves(terms)
    both = jnp.concatenate([high, low], axis=0).astype(BF16)
    summed = nt_dot(both, ohc[...])
    summed = (summed[0:8] + summed[8:16])[0:PARAMS]
    for o in range(2 * reach + 1):
        sendwin[o] = summed[:, o * E : (o + 1) * E]
    neighbours = -1
    for here in present:
        neighbours = neighbours + n_src * here.astype(jnp.int32)
    pl.semaphore_wait(barrier, neighbours)

    def window_copy(n):
        o, s = windows[n]
        return pltpu.make_async_remote_copy(
            src_ref=sendwin.at[o],
            dst_ref=recvwin.at[n],
            send_sem=wsend_sem.at[n],
            recv_sem=wrecv_sem.at[n],
            device_id={"dom": dom + offsets[o], "src": sources[s]},
            device_id_type=MESH,
        )

    count = range(len(windows))
    rising = [n for n in count if windows[n][0] >= reach]
    falling = [n for n in count if windows[n][0] < reach]
    for_each(rising, lambda n: windows[n][0], lambda n: window_copy(n).start())

    pool[QP:ROWS, :] = jnp.zeros((ROWS - QP, FACES), F32)
    for tile in range(5):
        wide = min(2, Q - 2 * tile)
        result = nn_dot(wt[...], v3[:, tile * 256 : tile * 256 + wide * E])
        for i in range(wide):
            q = 2 * tile + i
            for j in range(NF):
                pool[q * FP : (q + 1) * FP, j * E : (j + 1) * E] = result[
                    j * FP : (j + 1) * FP, i * E : (i + 1) * E
                ]
    high, low = halves(pool[...])
    pcat[:, 0:FACES] = high.astype(BF16)
    pcat[:, FACES : 2 * FACES] = low.astype(BF16)

    sendbuf[...] = nt_dot(ohs[...], pcat[:, 0:FACES]) + nt_dot(ohs[...], pcat[:, FACES : 2 * FACES])

    def trace_copy(k):
        part = pl.ds(k * cap, cap)
        return pltpu.make_async_remote_copy(
            src_ref=sendbuf.at[part],
            dst_ref=recvbuf.at[part],
            send_sem=send_sem.at[k],
            recv_sem=recv_sem.at[k],
            device_id={"dom": dom + offsets[goes[k]]},
            device_id_type=MESH,
        )

    for_each(range(slots), lambda k: goes[k], lambda k: trace_copy(k).start())
    for_each(falling, lambda n: windows[n][0], lambda n: window_copy(n).start())

    for i in (FLUX, NBR, ROT, LIFT, ORIENT, CLUS):
        loads[i].wait()

    def flux_side(j, side, values, finish):
        lanes = pl.ds(pl.multiple_of(j * E, E), E)
        x = [values[q * FP : (q + 1) * FP, lanes] for q in range(Q)]
        for p in range(Q):
            total = None
            for q in range(Q):
                term = flux_ref[j, p, q, side : side + 1, :] * x[q]
                total = term if total is None else total + term
            finish(j, p, total)

    def own_step(j, carry):
        def finish(j, p, total):
            ft[pl.ds(pl.multiple_of(j * FP, FP), FP), p * E : (p + 1) * E] = total

        flux_side(j, 0, pool, finish)
        return carry

    lax.fori_loop(0, NF, own_step, 0)

    build[...] = jnp.zeros_like(build)
    for d in range(3):
        high, low = halves(stiff_ref[d].T)
        build[d * B : (d + 1) * B, 0:B] = high
        build[d * B : (d + 1) * B, BP : BP + B] = high
        build[d * B : (d + 1) * B, 2 * BP : 2 * BP + B] = low
    wv[...] = build[0 : 3 * B, 0 : 3 * BP].astype(BF16)
    for group in range(3):
        multiply(wv, group, odd)

    def volume_step(block, carry):
        def finish(p, total):
            base[p] = adj_ref[0, p] + total

        contract(block, odd, finish)
        return carry

    lax.fori_loop(0, 3, volume_step, 0)

    for j in range(NF):
        row = lax.broadcasted_iota(jnp.int32, (FACES + slots * cap, E), 0)
        hit = row == nbr_ref[j : j + 1, :]
        oh[:, j * E : (j + 1) * E] = jnp.where(hit, 1.0, 0.0).astype(BF16)
    gath[...] = nn_dot(pcat[:, 0:FACES], oh[0:FACES, :]) + nn_dot(pcat[:, FACES : 2 * FACES], oh[0:FACES, :])

    build[...] = jnp.zeros_like(build)
    for o in range(3):
        high, low = halves(rot_ref[o])
        for i in range(3):
            rows = slice(i * 72 + o * FP, i * 72 + o * FP + F)
            build[rows, i * 72 : i * 72 + F] = high
            build[rows, i * 72 + FP : i * 72 + FP + F] = high
            build[rows, i * 72 + 2 * FP : i * 72 + 2 * FP + F] = low
    rb[...] = build[0:QP, 0:ROWS].astype(BF16)
    build[...] = jnp.zeros_like(build)
    for j in range(NF):
        high, low = halves(lift_ref[:, j, :].T)
        build[0:B, j * FP : j * FP + F] = high
        build[0:B, NF * FP + j * FP : NF * FP + j * FP + F] = high
        build[B : 2 * B, j * FP : j * FP + F] = low
    lw[...] = build[0 : 2 * B, 0 : 2 * NF * FP].astype(BF16)

    def no_faces(k):
        recvbuf[k * cap : (k + 1) * cap] = jnp.zeros((cap, ROWS), F32)

    for_each(range(slots), lambda k: comes[k], lambda k: trace_copy(k).wait_recv())
    for k in range(slots):

        @pl.when(jnp.logical_not(present[comes[k]]))
        def _():
            no_faces(k)

    high, low = halves(recvbuf[...].T)
    far = oh[FACES : FACES + slots * cap, :]
    gath[...] = gath[...] + nn_dot(high.astype(BF16), far) + nn_dot(low.astype(BF16), far)

    xg[QP:ROWS, :] = jnp.zeros((ROWS - QP, FACES), F32)
    for t in range(3):
        for i in range(3):
            q = 3 * t + i
            high, low = halves(gath[q * FP : (q + 1) * FP, :])
            xg[i * 72 : i * 72 + FP, :] = high
            xg[i * 72 + FP : i * 72 + 2 * FP, :] = low
            xg[i * 72 + 2 * FP : i * 72 + 3 * FP, :] = high
        result = nn_dot(rb[...], xg[...].astype(BF16))
        for i in range(3):
            q = 3 * t + i
            for j in range(NF):
                o = orient_ref[j : j + 1, :]
                r = [
                    result[i * 72 + n * FP : i * 72 + (n + 1) * FP, j * E : (j + 1) * E] for n in range(3)
                ]
                turned[q * FP : (q + 1) * FP, j * E : (j + 1) * E] = jnp.where(
                    o == 0, r[0], jnp.where(o == 1, r[1], r[2])
                )

    def far_step(j, carry):
        def finish(j, p, total):
            rows = pl.ds(pl.multiple_of(j * FP, FP), FP)
            lanes = slice(p * E, (p + 1) * E)
            ft[rows, lanes] = ft[rows, lanes] + total

        flux_side(j, 1, turned, finish)
        return carry

    lax.fori_loop(0, NF, far_step, 0)

    high, low = halves(ft[...])
    ftb[0 : NF * FP, :] = high.astype(BF16)
    ftb[NF * FP : 2 * NF * FP, :] = low.astype(BF16)
    moves = clus_ref[...] == 0
    for tile in range(5):
        wide = min(2, Q - 2 * tile)
        result = nn_dot(lw[...], ftb[:, tile * 256 : tile * 256 + wide * E])
        surface = result[0:B] + result[B : 2 * B]
        for i in range(wide):
            p = 2 * tile + i
            out_ref[0, p] = jnp.where(moves, base[p] - surface[:, i * E : (i + 1) * E], adj_ref[0, p])

    def no_window(n):
        recvwin[n] = jnp.zeros((PARAMS, E), F32)

    for_each(count, lambda n: 2 * reach - windows[n][0], lambda n: window_copy(n).wait_recv())
    for o in range(2 * reach + 1):

        @pl.when(jnp.logical_not(present[2 * reach - o]))
        def _():
            for n in count:
                if windows[n][0] == o:
                    no_window(n)

    total = sendwin[reach]
    for n in count:
        total = total + recvwin[n]
    grad_ref[...] = total

    for_each(range(slots), lambda k: goes[k], lambda k: trace_copy(k).wait_send())
    for_each(count, lambda n: windows[n][0], lambda n: window_copy(n).wait_send())


def store(next_ref, sums_ref, out_ref, grad_ref, sem):
    copies = [
        pltpu.make_async_copy(next_ref, out_ref, sem.at[0]),
        pltpu.make_async_copy(sums_ref, grad_ref, sem.at[1]),
    ]
    for copy in copies:
        copy.start()
    for copy in copies:
        copy.wait()


def solution(mesh):
    n_dom, n_src = mesh.shape["dom"], mesh.shape["src"]

    def body(adj, fwd, star, flux, stiff, restr, rot, lift, kw, nbr, send, orient, clus, cell):
        reach, cap = send.shape[0] // 2, send.shape[1]
        star = star.transpose(1, 2, 0, 3)
        flux = flux.transpose(0, 2, 3, 1, 4)
        restr = restr.transpose(2, 0, 1)
        lift = lift.transpose(1, 0, 2)
        kw = kw.transpose(1, 0, 2)
        slots = 2 * reach
        others = (slots + 1) * n_src - 1
        operands = (
            adj, fwd, star, flux, stiff, restr, rot, lift, kw, nbr, send, orient,
            clus.reshape(1, E), cell.reshape(1, E),
        )
        vmem = pl.BlockSpec(memory_space=pltpu.VMEM)
        dma = pltpu.SemaphoreType.DMA
        operands = tuple(pltpu.with_memory_space_constraint(x, pltpu.HBM) for x in operands)
        results = pl.pallas_call(
            functools.partial(kernel, n_dom, n_src, reach, cap),
            out_shape=(
                pltpu.VMEM(adj.shape, F32),
                pltpu.VMEM((PARAMS, E), F32),
            ),
            in_specs=[pl.BlockSpec(memory_space=pltpu.HBM)] * 14,
            out_specs=(vmem, vmem),
            scratch_shapes=[
                *[(pltpu.SMEM if i == KW else pltpu.VMEM)(x.shape, x.dtype) for i, x in enumerate(operands)],
                pltpu.VMEM((ROWS, 256), F32),
                pltpu.VMEM((3 * B, 3 * BP), BF16),
                pltpu.VMEM((3 * B, 3 * BP), BF16),
                pltpu.VMEM((NF * FP, 3 * BP), BF16),
                pltpu.VMEM((QP, ROWS), BF16),
                pltpu.VMEM((2 * B, 2 * NF * FP), BF16),
                pltpu.VMEM((3 * BP, Q * E), BF16),
                pltpu.VMEM((3, 3 * B, 3 * E), F32),
                pltpu.VMEM((3, 3 * B, 3 * E), F32),
                pltpu.VMEM((Q, B, E), F32),
                pltpu.VMEM((Q, B, E), F32),
                pltpu.VMEM((ROWS, FACES), F32),
                pltpu.VMEM((ROWS, 2 * FACES), BF16),
                pltpu.VMEM((FACES + slots * cap, FACES), BF16),
                pltpu.VMEM((slots * cap, FACES), BF16),
                pltpu.VMEM(((slots + 1) * E, E), BF16),
                pltpu.VMEM((ROWS, FACES), F32),
                pltpu.VMEM((ROWS, FACES), F32),
                pltpu.VMEM((QP, FACES), F32),
                pltpu.VMEM((NF * FP, Q * E), F32),
                pltpu.VMEM((2 * NF * FP, Q * E), BF16),
                pltpu.VMEM((Q, B, E), F32),
                pltpu.VMEM((slots * cap, ROWS), F32),
                pltpu.VMEM((slots * cap, ROWS), F32),
                pltpu.VMEM((slots + 1, PARAMS, E), F32),
                pltpu.VMEM((others, PARAMS, E), F32),
                dma((14,)),
                dma((slots,)),
                dma((slots,)),
                dma((others,)),
                dma((others,)),
            ],
            compiler_params=pltpu.CompilerParams(
                collective_id=0, has_side_effects=True, vmem_limit_bytes=32 * 1024 * 1024
            ),
        )(*operands)
        return pl.pallas_call(
            store,
            out_shape=(
                jax.ShapeDtypeStruct(adj.shape, F32),
                jax.ShapeDtypeStruct((PARAMS, E), F32),
            ),
            in_specs=[vmem, vmem],
            out_specs=[pl.BlockSpec(memory_space=pltpu.HBM)] * 2,
            scratch_shapes=[dma((2,))],
            compiler_params=pltpu.CompilerParams(vmem_limit_bytes=1024 * 1024),
        )(*(pltpu.with_memory_space_constraint(x, pltpu.VMEM) for x in results))

    placed = (
        P("src", None, None, "dom"),
        P("src", None, None, "dom"),
        P(None, None, None, "dom"),
        P(None, None, None, None, "dom"),
        P(),
        P(),
        P(),
        P(),
        P(),
        P(None, "dom"),
        P(None, "dom"),
        P(None, "dom"),
        P("dom"),
        P("dom"),
    )
    return jax.shard_map(
        body,
        mesh=mesh,
        in_specs=placed,
        out_specs=(P("src", None, None, "dom"), P(None, "dom")),
        check_vma=False,
    )
```

```python
import functools

import jax
import jax.numpy as jnp
from jax import lax
from jax.experimental import pallas as pl
from jax.experimental.pallas import tpu as pltpu
from jax.sharding import PartitionSpec as P

MESH = pl.DeviceIdType.MESH
F32 = jnp.float32
BF16 = jnp.bfloat16

Q = 9
B = 56
BP = 64
F = 21
FP = 24
E = 128
NF = 4
FACES = NF * E
ROWS = 224
QP = Q * FP
PARAMS = 3

ADJ, FWD, STAR, FLUX, STIFF, RESTR, ROT, LIFT, KW, NBR, SEND, ORIENT, CLUS, CELL = range(14)


def halves(x):
    high = x.astype(BF16).astype(F32)
    return high, x - high


def nt_dot(a, b):
    return lax.dot_general(a, b, (((1,), (1,)), ((), ())), preferred_element_type=F32)


def nn_dot(a, b):
    return jnp.dot(a, b, preferred_element_type=F32)


def kernel(
    n_dom,
    n_src,
    reach,
    cap,
    *refs,
):
    inputs, (out_ref, grad_ref), refs = refs[:14], refs[14:16], refs[16:]
    held, refs = refs[:14], refs[14:]
    (
        adj_ref, fwd_ref, star_ref, flux_ref, stiff_ref, restr_ref, rot_ref, lift_ref, kw_ref,
        nbr_ref, send_ref, orient_ref, clus_ref, cell_ref,
    ) = held
    (
    build,
    wk,
    wv,
    wt,
    rb,
    lw,
    v3,
    even,
    odd,
    integral,
    fwd32,
    pool,
    pcat,
    oh,
    ohs,
    ohc,
    gath,
    xg,
    turned,
    ft,
    ftb,
    base,
    sendbuf,
    recvbuf,
    sendwin,
    recvwin,
    load_sem,
    send_sem,
    recv_sem,
    wsend_sem,
    wrecv_sem,
    ) = refs
    dom = lax.axis_index("dom")
    src = lax.axis_index("src")
    slots = 2 * reach
    offsets = [o - reach for o in range(2 * reach + 1)]
    present = [(dom + d >= 0) & (dom + d < n_dom) for d in offsets]
    sources = [lax.rem(src + s, n_src) for s in range(n_src)]
    goes = [reach + k + 1 for k in range(reach)] + [reach - k - 1 for k in range(reach)]
    comes = [2 * reach - o for o in goes]
    windows = [(o, s) for o in range(2 * reach + 1) for s in range(n_src) if (o, s) != (reach, 0)]

    def for_each(keys, where, action):
        for o in reversed(range(2 * reach + 1)):
            mine = [k for k in keys if where(k) == o]
            if not mine:
                continue

            @pl.when(present[o])
            def _():
                for k in mine:
                    action(k)

    loads = [pltpu.make_async_copy(inputs[i], held[i], load_sem.at[i]) for i in range(14)]
    for i in (STIFF, ADJ, STAR, RESTR, SEND, CELL):
        loads[i].start()

    barrier = pltpu.get_barrier_semaphore()

    def greet(key):
        o, s = key
        pl.semaphore_signal(
            barrier, inc=1, device_id={"dom": dom + offsets[o], "src": sources[s]}, device_id_type=MESH
        )

    for_each(windows, lambda key: key[0], greet)

    build[...] = jnp.zeros_like(build)
    loads[STIFF].wait()
    for d in range(3):
        high, low = halves(stiff_ref[d])
        build[d * B : (d + 1) * B, 0:B] = high
        build[d * B : (d + 1) * B, BP : BP + B] = high
        build[d * B : (d + 1) * B, 2 * BP : 2 * BP + B] = low
    wk[...] = build[0 : 3 * B, 0 : 3 * BP].astype(BF16)

    loads[RESTR].wait()
    build[...] = jnp.zeros_like(build)
    for j in range(NF):
        high, low = halves(restr_ref[:, j, :])
        build[j * FP : j * FP + F, 0:B] = high
        build[j * FP : j * FP + F, BP : BP + B] = high
        build[j * FP : j * FP + F, 2 * BP : 2 * BP + B] = low
    wt[...] = build[0 : NF * FP, 0 : 3 * BP].astype(BF16)
    loads[SEND].wait()
    listed = send_ref[...].astype(F32).T
    face_lane = lax.broadcasted_iota(jnp.int32, (cap, FACES), 1).astype(F32)
    for k in range(slots):
        hit = listed[:, k : k + 1] == face_lane
        hit = jnp.where(hit, 1.0, 0.0).astype(BF16)
        ohs[k * cap : (k + 1) * cap, 0:FACES] = hit
        ohs[k * cap : (k + 1) * cap, FACES : 2 * FACES] = hit
    loads[CELL].wait()
    place = cell_ref[...] - (dom - reach) * E
    row = lax.broadcasted_iota(jnp.int32, ((2 * reach + 1) * E, E), 0)
    ohc[...] = jnp.where(row == place, 1.0, 0.0).astype(BF16)

    zeros8 = jnp.zeros((BP - B, E), F32)

    def put_state(q, value):
        high, low = halves(jnp.concatenate([value, zeros8], axis=0))
        lanes = pl.ds(pl.multiple_of(q * E, E), E)
        v3[0:BP, lanes] = high.astype(BF16)
        v3[BP : 2 * BP, lanes] = low.astype(BF16)
        v3[2 * BP : 3 * BP, lanes] = high.astype(BF16)

    def start_state(q, carry):
        value = adj_ref[0, q]
        integral[q] = value
        put_state(q, value)
        return carry

    loads[ADJ].wait()
    lax.fori_loop(0, Q, start_state, 0)
    loads[STAR].wait()
    for i in (FWD, KW, FLUX, NBR, ROT, LIFT, ORIENT, CLUS):
        loads[i].start()

    def multiply(weights, group, target):
        lanes = pl.ds(pl.multiple_of(group * 3 * E, E), 3 * E)
        target[group] = nn_dot(weights[...], v3[:, lanes])

    def contract(block, source, finish):
        totals = [None] * 3
        for q in range(Q):
            for d in range(3):
                a = source[q // 3, d * B : (d + 1) * B, (q % 3) * E : (q % 3 + 1) * E]
                for i in range(3):
                    term = star_ref[3 * block + i, q, d : d + 1, :] * a
                    totals[i] = term if totals[i] is None else totals[i] + term
        for i in range(3):
            finish(3 * block + i, totals[i])

    def degree_step(scale, now, later):
        def finish(p, total):
            value = total * scale
            integral[p] = integral[p] + value
            put_state(p, integral[p] if later is None else value)

        multiply(wk, 2, now)
        contract(0, now, finish)

        def block_step(block, c):
            if later is not None:
                multiply(wk, block - 1, later)
            contract(block, now, finish)
            return c

        lax.fori_loop(1, 3, block_step, 0)

    multiply(wk, 0, even)
    multiply(wk, 1, even)

    def two_degrees(k, carry):
        degree_step(jnp.where(k == 0, jnp.float32(-1 / 2), jnp.float32(-1 / 4)), even, odd)
        degree_step(jnp.where(k == 0, jnp.float32(-1 / 3), jnp.float32(-1 / 5)), odd, even)
        return carry

    lax.fori_loop(0, 2, two_degrees, 0)
    degree_step(jnp.float32(-1 / 6), even, None)

    for i in (FWD, KW):
        loads[i].wait()
    fwd32[...] = fwd_ref[0].astype(F32)

    def pair_step(q, carry):
        own = integral[q]
        sums = list(carry)
        for r in range(Q):
            product = own * fwd32[r]
            pair = product[0:8]
            for c in range(1, 7):
                pair = pair + product[8 * c : 8 * c + 8]
            for n in range(PARAMS):
                sums[n] = sums[n] + kw_ref[q, n, r] * pair
        return tuple(sums)

    sums = lax.fori_loop(0, Q, pair_step, tuple(jnp.zeros((8, E), F32) for _ in range(PARAMS)))
    terms = jnp.concatenate(
        [jnp.sum(s, axis=0, keepdims=True) for s in sums] + [jnp.zeros((8 - PARAMS, E), F32)], axis=0
    )
    high, low = halves(terms)
    both = jnp.concatenate([high, low], axis=0).astype(BF16)
    summed = nt_dot(both, ohc[...])
    summed = (summed[0:8] + summed[8:16])[0:PARAMS]
    for o in range(2 * reach + 1):
        sendwin[o] = summed[:, o * E : (o + 1) * E]
    neighbours = -1
    for here in present:
        neighbours = neighbours + n_src * here.astype(jnp.int32)
    pl.semaphore_wait(barrier, neighbours)

    def window_copy(n):
        o, s = windows[n]
        return pltpu.make_async_remote_copy(
            src_ref=sendwin.at[o],
            dst_ref=recvwin.at[n],
            send_sem=wsend_sem.at[n],
            recv_sem=wrecv_sem.at[n],
            device_id={"dom": dom + offsets[o], "src": sources[s]},
            device_id_type=MESH,
        )

    count = range(len(windows))
    rising = [n for n in count if windows[n][0] > reach]
    falling = [n for n in count if windows[n][0] <= reach]
    for_each(rising, lambda n: windows[n][0], lambda n: window_copy(n).start())

    pool[QP:ROWS, :] = jnp.zeros((ROWS - QP, FACES), F32)
    for tile in range(5):
        wide = min(2, Q - 2 * tile)
        result = nn_dot(wt[...], v3[:, tile * 256 : tile * 256 + wide * E])
        for i in range(wide):
            q = 2 * tile + i
            for j in range(NF):
                pool[q * FP : (q + 1) * FP, j * E : (j + 1) * E] = result[
                    j * FP : (j + 1) * FP, i * E : (i + 1) * E
                ]
    high, low = halves(pool[...])
    pcat[:, 0:FACES] = high.astype(BF16)
    pcat[:, FACES : 2 * FACES] = low.astype(BF16)

    sendbuf[...] = nt_dot(ohs[...], pcat[...])

    def trace_copy(k):
        part = pl.ds(k * cap, cap)
        return pltpu.make_async_remote_copy(
            src_ref=sendbuf.at[part],
            dst_ref=recvbuf.at[part],
            send_sem=send_sem.at[k],
            recv_sem=recv_sem.at[k],
            device_id={"dom": dom + offsets[goes[k]]},
            device_id_type=MESH,
        )

    for_each(range(slots), lambda k: goes[k], lambda k: trace_copy(k).start())
    for_each(falling, lambda n: windows[n][0], lambda n: window_copy(n).start())

    for i in (FLUX, NBR, ROT, LIFT, ORIENT, CLUS):
        loads[i].wait()

    def flux_side(j, side, values, finish):
        lanes = pl.ds(pl.multiple_of(j * E, E), E)
        x = [values[q * FP : (q + 1) * FP, lanes] for q in range(Q)]
        for p in range(Q):
            total = None
            for q in range(Q):
                term = flux_ref[j, p, q, side : side + 1, :] * x[q]
                total = term if total is None else total + term
            finish(j, p, total)

    def own_step(j, carry):
        def finish(j, p, total):
            ft[pl.ds(pl.multiple_of(j * FP, FP), FP), p * E : (p + 1) * E] = total

        flux_side(j, 0, pool, finish)
        return carry

    lax.fori_loop(0, NF, own_step, 0)

    build[...] = jnp.zeros_like(build)
    for d in range(3):
        high, low = halves(stiff_ref[d].T)
        build[d * B : (d + 1) * B, 0:B] = high
        build[d * B : (d + 1) * B, BP : BP + B] = high
        build[d * B : (d + 1) * B, 2 * BP : 2 * BP + B] = low
    wv[...] = build[0 : 3 * B, 0 : 3 * BP].astype(BF16)
    for group in range(3):
        multiply(wv, group, odd)

    def volume_step(block, carry):
        def finish(p, total):
            base[p] = adj_ref[0, p] + total

        contract(block, odd, finish)
        return carry

    lax.fori_loop(0, 3, volume_step, 0)

    for j in range(NF):
        row = lax.broadcasted_iota(jnp.int32, (FACES + slots * cap, E), 0)
        hit = row == nbr_ref[j : j + 1, :]
        oh[:, j * E : (j + 1) * E] = jnp.where(hit, 1.0, 0.0).astype(BF16)
    gath[...] = nn_dot(pcat[:, 0:FACES], oh[0:FACES, :]) + nn_dot(pcat[:, FACES : 2 * FACES], oh[0:FACES, :])

    build[...] = jnp.zeros_like(build)
    for o in range(3):
        high, low = halves(rot_ref[o])
        for i in range(3):
            rows = slice(i * 72 + o * FP, i * 72 + o * FP + F)
            build[rows, i * 72 : i * 72 + F] = high
            build[rows, i * 72 + FP : i * 72 + FP + F] = high
            build[rows, i * 72 + 2 * FP : i * 72 + 2 * FP + F] = low
    rb[...] = build[0:QP, 0:ROWS].astype(BF16)
    build[...] = jnp.zeros_like(build)
    for j in range(NF):
        high, low = halves(lift_ref[:, j, :].T)
        build[0:B, j * FP : j * FP + F] = high
        build[0:B, NF * FP + j * FP : NF * FP + j * FP + F] = high
        build[B : 2 * B, j * FP : j * FP + F] = low
    lw[...] = build[0 : 2 * B, 0 : 2 * NF * FP].astype(BF16)

    def no_faces(k):
        recvbuf[k * cap : (k + 1) * cap] = jnp.zeros((cap, ROWS), F32)

    for_each(range(slots), lambda k: comes[k], lambda k: trace_copy(k).wait_recv())
    for k in range(slots):

        @pl.when(jnp.logical_not(present[comes[k]]))
        def _():
            no_faces(k)

    high, low = halves(recvbuf[...].T)
    far = oh[FACES : FACES + slots * cap, :]
    gath[...] = gath[...] + nn_dot(high.astype(BF16), far) + nn_dot(low.astype(BF16), far)

    xg[QP:ROWS, :] = jnp.zeros((ROWS - QP, FACES), F32)
    for t in range(3):
        for i in range(3):
            q = 3 * t + i
            high, low = halves(gath[q * FP : (q + 1) * FP, :])
            xg[i * 72 : i * 72 + FP, :] = high
            xg[i * 72 + FP : i * 72 + 2 * FP, :] = low
            xg[i * 72 + 2 * FP : i * 72 + 3 * FP, :] = high
        result = nn_dot(rb[...], xg[...].astype(BF16))
        for i in range(3):
            q = 3 * t + i
            for j in range(NF):
                o = orient_ref[j : j + 1, :]
                r = [
                    result[i * 72 + n * FP : i * 72 + (n + 1) * FP, j * E : (j + 1) * E] for n in range(3)
                ]
                turned[q * FP : (q + 1) * FP, j * E : (j + 1) * E] = jnp.where(
                    o == 0, r[0], jnp.where(o == 1, r[1], r[2])
                )

    def far_step(j, carry):
        def finish(j, p, total):
            rows = pl.ds(pl.multiple_of(j * FP, FP), FP)
            lanes = slice(p * E, (p + 1) * E)
            ft[rows, lanes] = ft[rows, lanes] + total

        flux_side(j, 1, turned, finish)
        return carry

    lax.fori_loop(0, NF, far_step, 0)

    high, low = halves(ft[...])
    ftb[0 : NF * FP, :] = high.astype(BF16)
    ftb[NF * FP : 2 * NF * FP, :] = low.astype(BF16)
    moves = clus_ref[...] == 0
    for tile in range(5):
        wide = min(2, Q - 2 * tile)
        result = nn_dot(lw[...], ftb[:, tile * 256 : tile * 256 + wide * E])
        surface = result[0:B] + result[B : 2 * B]
        for i in range(wide):
            p = 2 * tile + i
            out_ref[0, p] = jnp.where(moves, base[p] - surface[:, i * E : (i + 1) * E], adj_ref[0, p])

    def no_window(n):
        recvwin[n] = jnp.zeros((PARAMS, E), F32)

    for_each(count, lambda n: 2 * reach - windows[n][0], lambda n: window_copy(n).wait_recv())
    for o in range(2 * reach + 1):

        @pl.when(jnp.logical_not(present[2 * reach - o]))
        def _():
            for n in count:
                if windows[n][0] == o:
                    no_window(n)

    total = sendwin[reach]
    for n in count:
        total = total + recvwin[n]
    grad_ref[...] = total

    for_each(range(slots), lambda k: goes[k], lambda k: trace_copy(k).wait_send())
    for_each(count, lambda n: windows[n][0], lambda n: window_copy(n).wait_send())


def store(next_ref, sums_ref, out_ref, grad_ref, sem):
    copies = [
        pltpu.make_async_copy(next_ref, out_ref, sem.at[0]),
        pltpu.make_async_copy(sums_ref, grad_ref, sem.at[1]),
    ]
    for copy in copies:
        copy.start()
    for copy in copies:
        copy.wait()


def solution(mesh):
    n_dom, n_src = mesh.shape["dom"], mesh.shape["src"]

    def body(adj, fwd, star, flux, stiff, restr, rot, lift, kw, nbr, send, orient, clus, cell):
        reach, cap = send.shape[0] // 2, send.shape[1]
        star = star.transpose(1, 2, 0, 3)
        flux = flux.transpose(0, 2, 3, 1, 4)
        restr = restr.transpose(2, 0, 1)
        lift = lift.transpose(1, 0, 2)
        kw = kw.transpose(1, 0, 2)
        slots = 2 * reach
        others = (slots + 1) * n_src - 1
        operands = (
            adj, fwd, star, flux, stiff, restr, rot, lift, kw, nbr, send, orient,
            clus.reshape(1, E), cell.reshape(1, E),
        )
        vmem = pl.BlockSpec(memory_space=pltpu.VMEM)
        dma = pltpu.SemaphoreType.DMA
        operands = tuple(pltpu.with_memory_space_constraint(x, pltpu.HBM) for x in operands)
        results = pl.pallas_call(
            functools.partial(kernel, n_dom, n_src, reach, cap),
            out_shape=(
                pltpu.VMEM(adj.shape, F32),
                pltpu.VMEM((PARAMS, E), F32),
            ),
            in_specs=[pl.BlockSpec(memory_space=pltpu.HBM)] * 14,
            out_specs=(vmem, vmem),
            scratch_shapes=[
                *[(pltpu.SMEM if i == KW else pltpu.VMEM)(x.shape, x.dtype) for i, x in enumerate(operands)],
                pltpu.VMEM((ROWS, 256), F32),
                pltpu.VMEM((3 * B, 3 * BP), BF16),
                pltpu.VMEM((3 * B, 3 * BP), BF16),
                pltpu.VMEM((NF * FP, 3 * BP), BF16),
                pltpu.VMEM((QP, ROWS), BF16),
                pltpu.VMEM((2 * B, 2 * NF * FP), BF16),
                pltpu.VMEM((3 * BP, Q * E), BF16),
                pltpu.VMEM((3, 3 * B, 3 * E), F32),
                pltpu.VMEM((3, 3 * B, 3 * E), F32),
                pltpu.VMEM((Q, B, E), F32),
                pltpu.VMEM((Q, B, E), F32),
                pltpu.VMEM((ROWS, FACES), F32),
                pltpu.VMEM((ROWS, 2 * FACES), BF16),
                pltpu.VMEM((FACES + slots * cap, FACES), BF16),
                pltpu.VMEM((slots * cap, 2 * FACES), BF16),
                pltpu.VMEM(((slots + 1) * E, E), BF16),
                pltpu.VMEM((ROWS, FACES), F32),
                pltpu.VMEM((ROWS, FACES), F32),
                pltpu.VMEM((QP, FACES), F32),
                pltpu.VMEM((NF * FP, Q * E), F32),
                pltpu.VMEM((2 * NF * FP, Q * E), BF16),
                pltpu.VMEM((Q, B, E), F32),
                pltpu.VMEM((slots * cap, ROWS), F32),
                pltpu.VMEM((slots * cap, ROWS), F32),
                pltpu.VMEM((slots + 1, PARAMS, E), F32),
                pltpu.VMEM((others, PARAMS, E), F32),
                dma((14,)),
                dma((slots,)),
                dma((slots,)),
                dma((others,)),
                dma((others,)),
            ],
            compiler_params=pltpu.CompilerParams(
                collective_id=0, has_side_effects=True, vmem_limit_bytes=32 * 1024 * 1024
            ),
        )(*operands)
        return pl.pallas_call(
            store,
            out_shape=(
                jax.ShapeDtypeStruct(adj.shape, F32),
                jax.ShapeDtypeStruct((PARAMS, E), F32),
            ),
            in_specs=[vmem, vmem],
            out_specs=[pl.BlockSpec(memory_space=pltpu.HBM)] * 2,
            scratch_shapes=[dma((2,))],
            compiler_params=pltpu.CompilerParams(vmem_limit_bytes=1024 * 1024),
        )(*(pltpu.with_memory_space_constraint(x, pltpu.VMEM) for x in results))

    placed = (
        P("src", None, None, "dom"),
        P("src", None, None, "dom"),
        P(None, None, None, "dom"),
        P(None, None, None, None, "dom"),
        P(),
        P(),
        P(),
        P(),
        P(),
        P(None, "dom"),
        P(None, "dom"),
        P(None, "dom"),
        P("dom"),
        P("dom"),
    )
    return jax.shard_map(
        body,
        mesh=mesh,
        in_specs=placed,
        out_specs=(P("src", None, None, "dom"), P(None, "dom")),
        check_vma=False,
    )
```
